256 devices in a mesh: col: 32 (over x, y, core), rep: 8 (over z).
Axes of the slice: x: 4, y: 4, z: 8, core: 2. Of those that a mesh axis runs over, the one named last changes fastest.
Arguments:
- gradient: bfloat16 [8, 4096, 16384], P('rep', None, 'col'), as said below
- error: bfloat16 [8, 4096, 16384], P('rep', None, 'col'), may hold values from -3 to 3
- warm_start: bfloat16 [32, 16384], P(None, 'col'), as said below
Outputs:
- new_error: bfloat16 [8, 4096, 16384], P('rep', None, 'col')
- q_factor: float32 [32, 16384], P(None, 'col')
The draws below stay inside these ranges and needn't reach their ends.
Inputs may be any that keep to these rules, and one draw needn't show every extreme that they name: `gradient`: finite values. `warm_start`: finite values.
All inputs are finite; a program needn't handle non-finite values.
Results may differ from the reference program's by a relative error of at most 0.012.
Values may be sent and summed in bfloat16 or wider, within the bound.
No kernel may reach another device: no remote copies, remote signals or barrier semaphores. Data moves between devices by JAX's collectives and lax.ppermute only.
A program may use at most 64 MiB of HBM per device.

```python
import math
import jax
import jax.numpy as jnp
from jax import lax

D = 4096
RANK = 32
COLS = 16384
REPS = 8


def draw_gradient(key, part):
    key = jax.random.fold_in(key, 11)
    key_scale, key_noise = jax.random.split(key, 2)
    row_scale = jnp.exp(jax.random.uniform(key_scale, (REPS, D, 1), jnp.float32) * math.log(10.0))
    noise = jnp.clip(jax.random.normal(key_noise, (REPS, D, COLS), jnp.float32), -6.0, 6.0)
    return (row_scale * noise).astype(jnp.bfloat16)


def draw_warm_start(key, part):
    key = jax.random.fold_in(key, 23)
    key_scale, key_noise = jax.random.split(key)
    rank_scale = jnp.exp(jax.random.uniform(key_scale, (RANK, 1), jnp.float32) * math.log(10.0))
    noise = jnp.clip(jax.random.normal(key_noise, (RANK, COLS), jnp.float32), -6.0, 6.0)
    return (rank_scale * noise / math.sqrt(COLS)).astype(jnp.bfloat16)


def levels(key, dims, cuts, least, high):
    factor_of = 1.0
    for position, blocks in cuts:
        steps = jax.random.uniform(jax.random.fold_in(jax.random.fold_in(key, 6), position), (blocks,), jnp.float32, least / len(cuts), high / len(cuts))
        factor_of = factor_of * jnp.repeat(jnp.exp(steps), dims[position] // blocks).reshape((-1,) + (1,) * (len(dims) - 1 - position))
    return factor_of


def centred(rng, dims, spread, most, cuts=(), held_as=jnp.bfloat16):
    result = spread * jax.random.normal(rng, dims, jnp.float32)
    if cuts:
        result = result * levels(rng, dims, cuts, -0.22, 0.18)
    return jnp.clip(result, -most, most).astype(held_as)


def setup_inputs(seed: int = 0) -> dict:
    key_of = jax.random.split(jax.random.key(seed), 4)
    return {
        "gradient": draw_gradient(jax.random.fold_in(key_of[3], 71), 0),
        "error": centred(key_of[1], (REPS, D, COLS), 0.5, 3.0, ((0, 8), (2, 32))),
        "warm_start": draw_warm_start(jax.random.fold_in(key_of[3], 71), 0),
    }


def merge_one(gradient, error, index):
    return (gradient[index].astype(jnp.float32) + error[index].astype(jnp.float32)).astype(jnp.bfloat16)

def reference(gradient, error, warm_start):
    p_sum = jnp.zeros((RANK, D), jnp.float32)
    for index in range(REPS):
        merged = merge_one(gradient, error, index)
        p_sum = p_sum + lax.dot_general(warm_start.astype(jnp.float32), merged.astype(jnp.float32), (((1,), (1,)), ((), ())), preferred_element_type=jnp.float32)
    gram = jnp.dot(p_sum, p_sum.T, precision=lax.Precision.HIGHEST)
    lower = jnp.linalg.cholesky(gram)
    basis = jax.scipy.linalg.solve_triangular(lower, p_sum, lower=True).astype(jnp.bfloat16)
    q_acc = jnp.zeros((RANK, COLS), jnp.float32)
    for index in range(REPS):
        merged = merge_one(gradient, error, index)
        q_acc = q_acc + jnp.dot(basis.astype(jnp.float32), merged.astype(jnp.float32), preferred_element_type=jnp.float32)
    q_factor = q_acc / REPS
    q_round = q_factor.astype(jnp.bfloat16)
    outputs = []
    for index in range(REPS):
        merged = merge_one(gradient, error, index)
        rebuilt = lax.dot_general(basis.astype(jnp.float32), q_round.astype(jnp.float32), (((0,), (0,)), ((), ())), preferred_element_type=jnp.float32)
        outputs.append((merged.astype(jnp.float32) - rebuilt).astype(jnp.bfloat16))
    return (jnp.stack(outputs), q_factor)
```

```python
import jax
import jax.numpy as jnp
from jax import lax
from jax.sharding import PartitionSpec as P

BF16, F32 = jnp.bfloat16, jnp.float32
WIDTH = 128


def exchange(blocks, axis):
    return lax.all_to_all(blocks, axis, 0, 0, tiled=True)


def share(block, axis):
    return exchange(jnp.broadcast_to(block[None], (lax.axis_size(axis),) + block.shape), axis)


def total(blocks):
    return jnp.sum(blocks.astype(F32), axis=0)


def per_device(gradient, error, warm_start):
    rank, rows = warm_start.shape[0], gradient.shape[1]
    merged = (gradient[0].astype(F32) + error[0].astype(F32)).astype(BF16)
    part = lax.dot_general(warm_start, merged, (((1,), (1,)), ((), ())), preferred_element_type=F32)
    blocks = part.reshape(rank, rows // WIDTH, WIDTH).transpose(1, 0, 2)
    with jax.named_scope("left_factor"):
        own = total(exchange(blocks.astype(BF16), "col"))
        own = total(share(own, "rep"))
        p_sum = share(own.astype(BF16), "col").transpose(1, 0, 2).reshape(rank, rows)
    gram = lax.dot_general(p_sum, p_sum, (((1,), (1,)), ((), ())), preferred_element_type=F32)
    lower = jnp.linalg.cholesky(gram)
    inverse = jax.scipy.linalg.solve_triangular(lower, jnp.eye(rank, dtype=F32), lower=True)
    raw = jnp.dot(p_sum, merged, preferred_element_type=F32)
    raw = total(share(raw.astype(BF16), "rep"))
    q_factor = jnp.dot(inverse, raw, precision=lax.Precision.HIGHEST) / lax.axis_size("rep")
    q_round = q_factor.astype(BF16).astype(F32)
    solved = jnp.dot(inverse.T, q_round, precision=lax.Precision.HIGHEST)
    high = solved.astype(BF16)
    low = (solved - high.astype(F32)).astype(BF16)
    rebuilt = lax.dot_general(
        jnp.concatenate([p_sum, p_sum]), jnp.concatenate([high, low]), (((0,), (0,)), ((), ())), preferred_element_type=F32
    )
    new_error = (merged.astype(F32) - rebuilt).astype(BF16)
    return (new_error[None], q_factor)


def solution(mesh):
    in_specs = (P("rep", None, "col"), P("rep", None, "col"), P(None, "col"))
    out_specs = (P("rep", None, "col"), P(None, "col"))
    return jax.shard_map(
        per_device, mesh=mesh, in_specs=in_specs, out_specs=out_specs, check_vma=False
    )
```

```python
import jax
import jax.numpy as jnp
from jax import lax
from jax.experimental import pallas as pl
from jax.experimental.pallas import tpu as pltpu
from jax.sharding import PartitionSpec as P

BF16, F32 = jnp.bfloat16, jnp.float32
HIGHEST = lax.Precision.HIGHEST
LANES = 128
STEP = 512
WHOLE = pl.BlockSpec(memory_space=pltpu.VMEM)
ANYWHERE = pl.BlockSpec(memory_space=pl.ANY)


def params():
    return pltpu.CompilerParams(vmem_limit_bytes=40 << 20)


def in_vmem(array):
    return pltpu.with_memory_space_constraint(array, pltpu.VMEM)


def in_hbm(array):
    return pltpu.with_memory_space_constraint(array, pltpu.HBM)


def rows_of(chunk):
    return pl.ds(chunk * STEP, STEP)


def merge_kernel(gradient, error, warm, merged, part, gradient_in, error_in, warm_in, done):
    chunks = merged.shape[0] // STEP
    copies = [pltpu.make_async_copy(warm, warm_in, done.at[2 * chunks])]
    for chunk in range(chunks):
        here = rows_of(chunk)
        copies.append(pltpu.make_async_copy(gradient.at[0, here, :], gradient_in.at[here, :], done.at[2 * chunk]))
        copies.append(pltpu.make_async_copy(error.at[0, here, :], error_in.at[here, :], done.at[2 * chunk + 1]))
    for copy in copies:
        copy.start()
    copies[0].wait()
    for chunk in range(chunks):
        here = rows_of(chunk)
        copies[2 * chunk + 1].wait()
        copies[2 * chunk + 2].wait()
        value = (gradient_in[here, :].astype(F32) + error_in[here, :].astype(F32)).astype(BF16)
        merged[here, :] = value
        product = lax.dot_general(warm_in[...], value, (((1,), (1,)), ((), ())), preferred_element_type=F32)
        for block in range(STEP // LANES):
            part[chunk * (STEP // LANES) + block] = product[:, block * LANES : (block + 1) * LANES].astype(BF16)


def merge(gradient, error, warm):
    _, rows, columns = gradient.shape
    rank = warm.shape[0]
    return pl.pallas_call(
        merge_kernel,
        in_specs=[ANYWHERE] * 3,
        out_specs=[WHOLE, WHOLE],
        out_shape=[
            pltpu.VMEM((rows, columns), BF16),
            pltpu.VMEM((rows // LANES, rank, LANES), BF16),
        ],
        scratch_shapes=[
            pltpu.VMEM((rows, columns), BF16),
            pltpu.VMEM((rows, columns), BF16),
            pltpu.VMEM((rank, columns), BF16),
            pltpu.SemaphoreType.DMA((2 * (rows // STEP) + 1,)),
        ],
        compiler_params=params(),
        cost_estimate=pl.CostEstimate(flops=2 * rank * rows * columns, bytes_accessed=4 * rows * columns, transcendentals=0),
        name="merge",
    )(in_hbm(gradient), in_hbm(error), in_hbm(warm))


def side_by_side(blocks):
    return jnp.concatenate([blocks[i] for i in range(blocks.shape[0])], axis=1)


def raw_kernel(p_sum, merged, raw):
    value = jnp.dot(side_by_side(p_sum), merged[...], preferred_element_type=F32).astype(BF16)
    for copy in range(raw.shape[0]):
        raw[copy] = value


def raw_factor(p_sum, merged, copies):
    rows, columns = merged.shape
    rank = p_sum.shape[1]
    return pl.pallas_call(
        raw_kernel,
        in_specs=[WHOLE, WHOLE],
        out_specs=WHOLE,
        out_shape=pltpu.VMEM((copies, rank, columns), BF16),
        compiler_params=params(),
        cost_estimate=pl.CostEstimate(flops=2 * rank * rows * columns, bytes_accessed=2 * rows * columns, transcendentals=0),
        name="raw_factor",
    )(in_vmem(p_sum), in_vmem(merged))


def solve_kernel(p_sum, inverse, turned):
    rank = p_sum.shape[1]
    wide = side_by_side(p_sum)
    gram = lax.dot_general(wide, wide, (((1,), (1,)), ((), ())), preferred_element_type=F32)
    row = lax.broadcasted_iota(jnp.int32, (rank, rank), 0)
    col = lax.broadcasted_iota(jnp.int32, (rank, rank), 1)
    one = (row == col).astype(F32)
    table = jnp.concatenate([gram, one], axis=1)
    below = lax.broadcasted_iota(jnp.int32, (rank, 1), 0)
    for k in range(rank):
        pivot = table[k : k + 1, :]
        factor = jnp.where(below > k, table[:, k : k + 1] / pivot[:, k : k + 1], 0.0)
        table = table - factor * pivot
    diagonal = jnp.sum(table[:, :rank] * one, axis=1, keepdims=True)
    inverse[...] = table[:, rank:] * lax.rsqrt(diagonal)
    for block in range(p_sum.shape[0]):
        tall = p_sum[block].astype(F32).T.astype(BF16)
        turned[pl.ds(block * LANES, LANES), :] = jnp.concatenate([tall, tall], axis=1)


def solve(p_sum):
    blocks, rank, lanes = p_sum.shape
    return pl.pallas_call(
        solve_kernel,
        in_specs=[WHOLE],
        out_specs=[WHOLE, WHOLE],
        out_shape=[pltpu.VMEM((rank, rank), F32), pltpu.VMEM((blocks * lanes, 2 * rank), BF16)],
        compiler_params=params(),
        cost_estimate=pl.CostEstimate(flops=2 * rank * rank * blocks * lanes, bytes_accessed=2 << 20, transcendentals=0),
        name="solve",
    )(in_vmem(p_sum))


def finish_kernel(replicas, raw, inverse, turned, merged, new_error, q_factor, halves, result, done):
    total = jnp.sum(raw[...].astype(F32), axis=0)
    factor = jnp.dot(inverse[...], total, precision=HIGHEST, preferred_element_type=F32) * (1.0 / replicas)
    q_factor[...] = factor
    rounded = factor.astype(BF16).astype(F32)
    solved = lax.dot_general(
        inverse[...], rounded, (((0,), (0,)), ((), ())), precision=HIGHEST, preferred_element_type=F32
    )
    high = solved.astype(BF16)
    halves[...] = jnp.concatenate([high, (solved - high.astype(F32)).astype(BF16)], axis=0)
    copies = []
    for chunk in range(merged.shape[0] // STEP):
        here = rows_of(chunk)
        rebuilt = jnp.dot(turned[here, :], halves[...], preferred_element_type=F32)
        result[here, :] = (merged[here, :].astype(F32) - rebuilt).astype(BF16)
        copies.append(pltpu.make_async_copy(result.at[here, :], new_error.at[0, here, :], done.at[chunk]))
        copies[-1].start()
    for copy in copies:
        copy.wait()


def finish(raw, inverse, turned, merged, replicas):
    rows, columns = merged.shape
    rank = inverse.shape[0]
    return pl.pallas_call(
        lambda *refs: finish_kernel(replicas, *refs),
        in_specs=[WHOLE] * 4,
        out_specs=[ANYWHERE, WHOLE],
        out_shape=[
            pltpu.HBM((1, rows, columns), BF16),
            jax.ShapeDtypeStruct((rank, columns), F32),
        ],
        scratch_shapes=[
            pltpu.VMEM((2 * rank, columns), BF16),
            pltpu.VMEM((rows, columns), BF16),
            pltpu.SemaphoreType.DMA((rows // STEP,)),
        ],
        compiler_params=params(),
        cost_estimate=pl.CostEstimate(flops=4 * rank * rows * columns, bytes_accessed=4 * rows * columns, transcendentals=0),
        name="finish",
    )(in_vmem(raw), in_vmem(inverse), in_vmem(turned), in_vmem(merged))


def exchange(blocks, axis):
    return lax.all_to_all(blocks, axis, 0, 0, tiled=True)


def share(block, axis):
    return exchange(jnp.broadcast_to(block[None], (lax.axis_size(axis),) + block.shape), axis)


def total(blocks):
    return jnp.sum(blocks.astype(F32), axis=0)


def per_device(gradient, error, warm_start):
    replicas = lax.axis_size("rep")
    merged, part = merge(gradient, error, warm_start)
    own = total(exchange(part, "col"))
    own = total(share(own, "rep"))
    p_sum = share(own.astype(BF16), "col")
    raw = exchange(raw_factor(p_sum, merged, replicas), "rep")
    inverse, turned = solve(p_sum)
    return tuple(finish(raw, inverse, turned, merged, replicas))


def solution(mesh):
    in_specs = (P("rep", None, "col"), P("rep", None, "col"), P(None, "col"))
    out_specs = (P("rep", None, "col"), P(None, "col"))
    return jax.shard_map(
        per_device, mesh=mesh, in_specs=in_specs, out_specs=out_specs, check_vma=False
    )
```

```python
import jax
import jax.numpy as jnp
from jax import lax
from jax.experimental import pallas as pl
from jax.experimental.pallas import tpu as pltpu
from jax.sharding import PartitionSpec as P

BF16, F32 = jnp.bfloat16, jnp.float32
HIGHEST = lax.Precision.HIGHEST
LANES = 128
STEP = 512
WHOLE = pl.BlockSpec(memory_space=pltpu.VMEM)
ANYWHERE = pl.BlockSpec(memory_space=pl.ANY)


def params():
    return pltpu.CompilerParams(vmem_limit_bytes=40 << 20)


def in_vmem(array):
    return pltpu.with_memory_space_constraint(array, pltpu.VMEM)


def in_hbm(array):
    return pltpu.with_memory_space_constraint(array, pltpu.HBM)


def rows_of(chunk):
    return pl.ds(chunk * STEP, STEP)


def merge_kernel(gradient, error, warm, merged, part, gradient_in, error_in, warm_in, done):
    chunks = merged.shape[0] // STEP
    copies = [pltpu.make_async_copy(warm, warm_in, done.at[2 * chunks])]
    for chunk in range(chunks):
        here = rows_of(chunk)
        copies.append(pltpu.make_async_copy(gradient.at[0, here, :], gradient_in.at[here, :], done.at[2 * chunk]))
        copies.append(pltpu.make_async_copy(error.at[0, here, :], error_in.at[here, :], done.at[2 * chunk + 1]))
    for copy in copies:
        copy.start()
    copies[0].wait()
    for chunk in range(chunks):
        here = rows_of(chunk)
        copies[2 * chunk + 1].wait()
        copies[2 * chunk + 2].wait()
        value = (gradient_in[here, :].astype(F32) + error_in[here, :].astype(F32)).astype(BF16)
        merged[here, :] = value
        product = lax.dot_general(warm_in[...], value, (((1,), (1,)), ((), ())), preferred_element_type=F32)
        for block in range(STEP // LANES):
            part[chunk * (STEP // LANES) + block] = product[:, block * LANES : (block + 1) * LANES].astype(BF16)


def merge(gradient, error, warm):
    _, rows, columns = gradient.shape
    rank = warm.shape[0]
    return pl.pallas_call(
        merge_kernel,
        in_specs=[ANYWHERE] * 3,
        out_specs=[WHOLE, WHOLE],
        out_shape=[
            pltpu.VMEM((rows, columns), BF16),
            pltpu.VMEM((rows // LANES, rank, LANES), BF16),
        ],
        scratch_shapes=[
            pltpu.VMEM((rows, columns), BF16),
            pltpu.VMEM((rows, columns), BF16),
            pltpu.VMEM((rank, columns), BF16),
            pltpu.SemaphoreType.DMA((2 * (rows // STEP) + 1,)),
        ],
        compiler_params=params(),
        cost_estimate=pl.CostEstimate(flops=2 * rank * rows * columns, bytes_accessed=4 * rows * columns, transcendentals=0),
        name="merge",
    )(in_hbm(gradient), in_hbm(error), in_hbm(warm))


def side_by_side(blocks):
    return jnp.concatenate([blocks[i] for i in range(blocks.shape[0])], axis=1)


def factor_kernel(p_sum, merged, raw, inverse, turned):
    blocks, rank, lanes = p_sum.shape
    wide = side_by_side(p_sum)
    gram = lax.dot_general(wide, wide, (((1,), (1,)), ((), ())), preferred_element_type=F32)
    value = jnp.dot(wide, merged[...], preferred_element_type=F32).astype(BF16)
    for copy in range(raw.shape[0]):
        raw[copy] = value
    for block in range(blocks):
        tall = p_sum[block].astype(F32).T.astype(BF16)
        turned[pl.ds(block * lanes, lanes), :] = jnp.concatenate([tall, tall], axis=1)
    row = lax.broadcasted_iota(jnp.int32, (rank, rank), 0)
    col = lax.broadcasted_iota(jnp.int32, (rank, rank), 1)
    one = (row == col).astype(F32)
    table = jnp.concatenate([gram, one], axis=1)
    below = lax.broadcasted_iota(jnp.int32, (rank, 1), 0)
    for k in range(rank):
        pivot = table[k : k + 1, :]
        factor = jnp.where(below > k, table[:, k : k + 1] / pivot[:, k : k + 1], 0.0)
        table = table - factor * pivot
    diagonal = jnp.sum(table[:, :rank] * one, axis=1, keepdims=True)
    inverse[...] = table[:, rank:] * lax.rsqrt(diagonal)


def factor(p_sum, merged, copies):
    rows, columns = merged.shape
    rank = p_sum.shape[1]
    return pl.pallas_call(
        factor_kernel,
        in_specs=[WHOLE, WHOLE],
        out_specs=[WHOLE] * 3,
        out_shape=[
            pltpu.VMEM((copies, rank, columns), BF16),
            pltpu.VMEM((rank, rank), F32),
            pltpu.VMEM((rows, 2 * rank), BF16),
        ],
        compiler_params=params(),
        cost_estimate=pl.CostEstimate(flops=2 * rank * rows * columns, bytes_accessed=2 * rows * columns, transcendentals=0),
        name="factor",
    )(in_vmem(p_sum), in_vmem(merged))


def finish_kernel(replicas, raw, inverse, turned, merged, new_error, q_factor, halves, result, done):
    total = jnp.sum(raw[...].astype(F32), axis=0)
    factor = jnp.dot(inverse[...], total, precision=HIGHEST, preferred_element_type=F32) * (1.0 / replicas)
    q_factor[...] = factor
    rounded = factor.astype(BF16).astype(F32)
    solved = lax.dot_general(
        inverse[...], rounded, (((0,), (0,)), ((), ())), precision=HIGHEST, preferred_element_type=F32
    )
    high = solved.astype(BF16)
    halves[...] = jnp.concatenate([high, (solved - high.astype(F32)).astype(BF16)], axis=0)
    copies = []
    for chunk in range(merged.shape[0] // STEP):
        here = rows_of(chunk)
        rebuilt = jnp.dot(turned[here, :], halves[...], preferred_element_type=F32)
        result[here, :] = (merged[here, :].astype(F32) - rebuilt).astype(BF16)
        copies.append(pltpu.make_async_copy(result.at[here, :], new_error.at[0, here, :], done.at[chunk]))
        copies[-1].start()
    for copy in copies:
        copy.wait()


def finish(raw, inverse, turned, merged, replicas):
    rows, columns = merged.shape
    rank = inverse.shape[0]
    return pl.pallas_call(
        lambda *refs: finish_kernel(replicas, *refs),
        in_specs=[WHOLE] * 4,
        out_specs=[ANYWHERE, WHOLE],
        out_shape=[
            pltpu.HBM((1, rows, columns), BF16),
            jax.ShapeDtypeStruct((rank, columns), F32),
        ],
        scratch_shapes=[
            pltpu.VMEM((2 * rank, columns), BF16),
            pltpu.VMEM((rows, columns), BF16),
            pltpu.SemaphoreType.DMA((rows // STEP,)),
        ],
        compiler_params=params(),
        cost_estimate=pl.CostEstimate(flops=4 * rank * rows * columns, bytes_accessed=4 * rows * columns, transcendentals=0),
        name="finish",
    )(in_vmem(raw), in_vmem(inverse), in_vmem(turned), in_vmem(merged))


def exchange(blocks, axis):
    return lax.all_to_all(blocks, axis, 0, 0, tiled=True)


def share(block, axis):
    return exchange(jnp.broadcast_to(block[None], (lax.axis_size(axis),) + block.shape), axis)


def total(blocks):
    terms = [blocks[i].astype(F32) for i in range(blocks.shape[0])]
    while len(terms) > 1:
        terms = [a + b for a, b in zip(terms[::2], terms[1::2])]
    return terms[0]


def per_device(gradient, error, warm_start):
    replicas = lax.axis_size("rep")
    merged, part = merge(gradient, error, warm_start)
    own = total(exchange(part, "col"))
    own = total(share(own, "rep"))
    p_sum = share(own.astype(BF16), "col")
    raw, inverse, turned = factor(p_sum, merged, replicas)
    raw = exchange(raw, "rep")
    return tuple(finish(raw, inverse, turned, merged, replicas))


def solution(mesh):
    in_specs = (P("rep", None, "col"), P("rep", None, "col"), P(None, "col"))
    out_specs = (P("rep", None, "col"), P(None, "col"))
    return jax.shard_map(
        per_device, mesh=mesh, in_specs=in_specs, out_specs=out_specs, check_vma=False
    )
```

```python
import jax
import jax.numpy as jnp
from jax import lax
from jax.experimental import pallas as pl
from jax.experimental.pallas import tpu as pltpu
from jax.sharding import PartitionSpec as P

BF16, F32 = jnp.bfloat16, jnp.float32
HIGHEST = lax.Precision.HIGHEST
LANES = 128
STEP = 512
WHOLE = pl.BlockSpec(memory_space=pltpu.VMEM)
ANYWHERE = pl.BlockSpec(memory_space=pl.ANY)


def params():
    return pltpu.CompilerParams(vmem_limit_bytes=40 << 20)


def in_vmem(array):
    return pltpu.with_memory_space_constraint(array, pltpu.VMEM)


def in_hbm(array):
    return pltpu.with_memory_space_constraint(array, pltpu.HBM)


def rows_of(chunk):
    return pl.ds(chunk * STEP, STEP)


def merge_kernel(gradient, error, warm, merged, part, gradient_in, error_in, warm_in, done):
    chunks = merged.shape[0] // STEP
    copies = [pltpu.make_async_copy(warm, warm_in, done.at[2 * chunks])]
    for chunk in range(chunks):
        here = rows_of(chunk)
        copies.append(pltpu.make_async_copy(gradient.at[0, here, :], gradient_in.at[here, :], done.at[2 * chunk]))
        copies.append(pltpu.make_async_copy(error.at[0, here, :], error_in.at[here, :], done.at[2 * chunk + 1]))
    for copy in copies:
        copy.start()
    copies[0].wait()
    for chunk in range(chunks):
        here = rows_of(chunk)
        copies[2 * chunk + 1].wait()
        copies[2 * chunk + 2].wait()
        value = (gradient_in[here, :].astype(F32) + error_in[here, :].astype(F32)).astype(BF16)
        merged[here, :] = value
        product = lax.dot_general(warm_in[...], value, (((1,), (1,)), ((), ())), preferred_element_type=F32)
        for block in range(STEP // LANES):
            part[chunk * (STEP // LANES) + block] = product[:, block * LANES : (block + 1) * LANES].astype(BF16)


def merge(gradient, error, warm):
    _, rows, columns = gradient.shape
    rank = warm.shape[0]
    return pl.pallas_call(
        merge_kernel,
        in_specs=[ANYWHERE] * 3,
        out_specs=[WHOLE, WHOLE],
        out_shape=[
            pltpu.VMEM((rows, columns), BF16),
            pltpu.VMEM((rows // LANES, rank, LANES), BF16),
        ],
        scratch_shapes=[
            pltpu.VMEM((rows, columns), BF16),
            pltpu.VMEM((rows, columns), BF16),
            pltpu.VMEM((rank, columns), BF16),
            pltpu.SemaphoreType.DMA((2 * (rows // STEP) + 1,)),
        ],
        compiler_params=params(),
        cost_estimate=pl.CostEstimate(flops=2 * rank * rows * columns, bytes_accessed=4 * rows * columns, transcendentals=0),
        name="merge",
    )(in_hbm(gradient), in_hbm(error), in_hbm(warm))


def side_by_side(blocks):
    return jnp.concatenate([blocks[i] for i in range(blocks.shape[0])], axis=1)


def raw_kernel(p_sum, merged, raw):
    raw[...] = jnp.dot(side_by_side(p_sum), merged[...], preferred_element_type=F32).astype(BF16)


def raw_factor(p_sum, merged):
    rows, columns = merged.shape
    rank = p_sum.shape[1]
    return pl.pallas_call(
        raw_kernel,
        in_specs=[WHOLE, WHOLE],
        out_specs=WHOLE,
        out_shape=pltpu.VMEM((rank, columns), BF16),
        compiler_params=params(),
        cost_estimate=pl.CostEstimate(flops=2 * rank * rows * columns, bytes_accessed=2 * rows * columns, transcendentals=0),
        name="raw_factor",
    )(in_vmem(p_sum), in_vmem(merged))


def solve_kernel(p_sum, inverse, turned):
    blocks, rank, lanes = p_sum.shape
    wide = side_by_side(p_sum)
    gram = lax.dot_general(wide, wide, (((1,), (1,)), ((), ())), preferred_element_type=F32)
    for block in range(blocks):
        tall = p_sum[block].astype(F32).T.astype(BF16)
        turned[pl.ds(block * lanes, lanes), :] = jnp.concatenate([tall, tall], axis=1)
    row = lax.broadcasted_iota(jnp.int32, (rank, rank), 0)
    col = lax.broadcasted_iota(jnp.int32, (rank, rank), 1)
    one = (row == col).astype(F32)
    table = jnp.concatenate([gram, one], axis=1)
    below = lax.broadcasted_iota(jnp.int32, (rank, 1), 0)
    for k in range(rank):
        pivot = table[k : k + 1, :]
        factor = jnp.where(below > k, table[:, k : k + 1] / pivot[:, k : k + 1], 0.0)
        table = table - factor * pivot
    diagonal = jnp.sum(table[:, :rank] * one, axis=1, keepdims=True)
    inverse[...] = table[:, rank:] * lax.rsqrt(diagonal)


def solve(p_sum):
    blocks, rank, lanes = p_sum.shape
    return pl.pallas_call(
        solve_kernel,
        in_specs=[WHOLE],
        out_specs=[WHOLE, WHOLE],
        out_shape=[pltpu.VMEM((rank, rank), F32), pltpu.VMEM((blocks * lanes, 2 * rank), BF16)],
        compiler_params=params(),
        cost_estimate=pl.CostEstimate(flops=16 * rank * rank * blocks * lanes, bytes_accessed=4 << 20, transcendentals=0),
        name="solve",
    )(in_vmem(p_sum))


def finish_kernel(replicas, mine, theirs, inverse, turned, merged, new_error, q_factor, halves, result, done):
    raw = mine[...].astype(F32) + theirs[...].astype(F32)
    factor = jnp.dot(inverse[...], raw, precision=HIGHEST, preferred_element_type=F32) * (1.0 / replicas)
    q_factor[...] = factor
    rounded = factor.astype(BF16).astype(F32)
    solved = lax.dot_general(
        inverse[...], rounded, (((0,), (0,)), ((), ())), precision=HIGHEST, preferred_element_type=F32
    )
    high = solved.astype(BF16)
    halves[...] = jnp.concatenate([high, (solved - high.astype(F32)).astype(BF16)], axis=0)
    copies = []
    for chunk in range(merged.shape[0] // STEP):
        here = rows_of(chunk)
        rebuilt = jnp.dot(turned[here, :], halves[...], preferred_element_type=F32)
        result[here, :] = (merged[here, :].astype(F32) - rebuilt).astype(BF16)
        copies.append(pltpu.make_async_copy(result.at[here, :], new_error.at[0, here, :], done.at[chunk]))
        copies[-1].start()
    for copy in copies:
        copy.wait()


def finish(mine, theirs, inverse, turned, merged, replicas):
    rows, columns = merged.shape
    rank = inverse.shape[0]
    return pl.pallas_call(
        lambda *refs: finish_kernel(replicas, *refs),
        in_specs=[WHOLE] * 5,
        out_specs=[ANYWHERE, WHOLE],
        out_shape=[
            pltpu.HBM((1, rows, columns), BF16),
            jax.ShapeDtypeStruct((rank, columns), F32),
        ],
        scratch_shapes=[
            pltpu.VMEM((2 * rank, columns), BF16),
            pltpu.VMEM((rows, columns), BF16),
            pltpu.SemaphoreType.DMA((rows // STEP,)),
        ],
        compiler_params=params(),
        cost_estimate=pl.CostEstimate(flops=4 * rank * rows * columns, bytes_accessed=4 * rows * columns, transcendentals=0),
        name="finish",
    )(in_vmem(mine), in_vmem(theirs), in_vmem(inverse), in_vmem(turned), in_vmem(merged))


def exchange(blocks, axis):
    return lax.all_to_all(blocks, axis, 0, 0, tiled=True)


def share(block, axis):
    return exchange(jnp.broadcast_to(block[None], (lax.axis_size(axis),) + block.shape), axis)


def total(blocks):
    terms = [blocks[i].astype(F32) for i in range(blocks.shape[0])]
    while len(terms) > 1:
        terms = [a + b for a, b in zip(terms[::2], terms[1::2])]
    return terms[0]


def swap(block, axis, mask):
    return lax.ppermute(block, axis, [(i, i ^ mask) for i in range(lax.axis_size(axis))])


def per_device(gradient, error, warm_start):
    replicas = lax.axis_size("rep")
    merged, part = merge(gradient, error, warm_start)
    own = total(exchange(part, "col"))
    own = total(share(own, "rep"))
    p_sum = share(own.astype(BF16), "col")
    raw = raw_factor(p_sum, merged)
    inverse, turned = solve(p_sum)
    masks = [2**bit ^ (2 ** (bit - 1) if bit > 1 else 0) for bit in range(replicas.bit_length() - 1)]
    for mask in masks[:-1]:
        raw = (raw.astype(F32) + swap(raw, "rep", mask).astype(F32)).astype(BF16)
    return tuple(finish(raw, swap(raw, "rep", masks[-1]), inverse, turned, merged, replicas))


def solution(mesh):
    in_specs = (P("rep", None, "col"), P("rep", None, "col"), P(None, "col"))
    out_specs = (P("rep", None, "col"), P(None, "col"))
    return jax.shard_map(
        per_device, mesh=mesh, in_specs=in_specs, out_specs=out_specs, check_vma=False
    )
```

```python
import jax
import jax.numpy as jnp
from jax import lax
from jax.experimental import pallas as pl
from jax.experimental.pallas import tpu as pltpu
from jax.sharding import PartitionSpec as P

BF16, F32 = jnp.bfloat16, jnp.float32
HIGHEST = lax.Precision.HIGHEST
LANES = 128
STEP = 512
WHOLE = pl.BlockSpec(memory_space=pltpu.VMEM)
ANYWHERE = pl.BlockSpec(memory_space=pl.ANY)


def params():
    return pltpu.CompilerParams(vmem_limit_bytes=40 << 20)


def in_vmem(array):
    return pltpu.with_memory_space_constraint(array, pltpu.VMEM)


def in_hbm(array):
    return pltpu.with_memory_space_constraint(array, pltpu.HBM)


def rows_of(chunk):
    return pl.ds(chunk * STEP, STEP)


def merge_kernel(gradient, error, warm, merged, part, gradient_in, error_in, warm_in, done):
    chunks = merged.shape[0] // STEP
    copies = [pltpu.make_async_copy(warm, warm_in, done.at[2 * chunks])]
    for chunk in range(chunks):
        here = rows_of(chunk)
        copies.append(pltpu.make_async_copy(gradient.at[0, here, :], gradient_in.at[here, :], done.at[2 * chunk]))
        copies.append(pltpu.make_async_copy(error.at[0, here, :], error_in.at[here, :], done.at[2 * chunk + 1]))
    for copy in copies:
        copy.start()
    copies[0].wait()
    for chunk in range(chunks):
        here = rows_of(chunk)
        copies[2 * chunk + 1].wait()
        copies[2 * chunk + 2].wait()
        value = (gradient_in[here, :].astype(F32) + error_in[here, :].astype(F32)).astype(BF16)
        merged[here, :] = value
        product = lax.dot_general(warm_in[...], value, (((1,), (1,)), ((), ())), preferred_element_type=F32)
        for block in range(STEP // LANES):
            part[chunk * (STEP // LANES) + block] = product[:, block * LANES : (block + 1) * LANES].astype(BF16)


def merge(gradient, error, warm):
    _, rows, columns = gradient.shape
    rank = warm.shape[0]
    return pl.pallas_call(
        merge_kernel,
        in_specs=[ANYWHERE] * 3,
        out_specs=[WHOLE, WHOLE],
        out_shape=[
            pltpu.VMEM((rows, columns), BF16),
            pltpu.VMEM((rows // LANES, rank, LANES), BF16),
        ],
        scratch_shapes=[
            pltpu.VMEM((rows, columns), BF16),
            pltpu.VMEM((rows, columns), BF16),
            pltpu.VMEM((rank, columns), BF16),
            pltpu.SemaphoreType.DMA((2 * (rows // STEP) + 1,)),
        ],
        compiler_params=params(),
        cost_estimate=pl.CostEstimate(flops=2 * rank * rows * columns, bytes_accessed=4 * rows * columns, transcendentals=0),
        name="merge",
    )(in_hbm(gradient), in_hbm(error), in_hbm(warm))


def side_by_side(blocks):
    return jnp.concatenate([blocks[i] for i in range(blocks.shape[0])], axis=1)


def raw_kernel(p_sum, merged, raw):
    raw[...] = jnp.dot(side_by_side(p_sum), merged[...], preferred_element_type=F32).astype(BF16)


def raw_factor(p_sum, merged):
    rows, columns = merged.shape
    rank = p_sum.shape[1]
    return pl.pallas_call(
        raw_kernel,
        in_specs=[WHOLE, WHOLE],
        out_specs=WHOLE,
        out_shape=pltpu.VMEM((rank, columns), BF16),
        compiler_params=params(),
        cost_estimate=pl.CostEstimate(flops=2 * rank * rows * columns, bytes_accessed=2 * rows * columns, transcendentals=0),
        name="raw_factor",
    )(in_vmem(p_sum), in_vmem(merged))


def solve_kernel(p_sum, inverse, turned):
    blocks, rank, lanes = p_sum.shape
    wide = side_by_side(p_sum)
    gram = lax.dot_general(wide, wide, (((1,), (1,)), ((), ())), preferred_element_type=F32)
    for block in range(blocks):
        tall = p_sum[block].astype(F32).T.astype(BF16)
        turned[pl.ds(block * lanes, lanes), :] = jnp.concatenate([tall, tall], axis=1)
    row = lax.broadcasted_iota(jnp.int32, (rank, rank), 0)
    col = lax.broadcasted_iota(jnp.int32, (rank, rank), 1)
    one = (row == col).astype(F32)
    table = jnp.concatenate([gram, one], axis=1)
    below = lax.broadcasted_iota(jnp.int32, (rank, 1), 0)
    for k in range(rank):
        pivot = table[k : k + 1, :]
        factor = jnp.where(below > k, table[:, k : k + 1] / pivot[:, k : k + 1], 0.0)
        table = table - factor * pivot
    diagonal = jnp.sum(table[:, :rank] * one, axis=1, keepdims=True)
    inverse[...] = table[:, rank:] * lax.rsqrt(diagonal)


def solve(p_sum):
    blocks, rank, lanes = p_sum.shape
    return pl.pallas_call(
        solve_kernel,
        in_specs=[WHOLE],
        out_specs=[WHOLE, WHOLE],
        out_shape=[pltpu.VMEM((rank, rank), F32), pltpu.VMEM((blocks * lanes, 2 * rank), BF16)],
        compiler_params=params(),
        cost_estimate=pl.CostEstimate(flops=16 * rank * rank * blocks * lanes, bytes_accessed=4 << 20, transcendentals=0),
        name="solve",
    )(in_vmem(p_sum))


def finish_kernel(replicas, mine, theirs, inverse, turned, merged, new_error, q_factor, halves, result, done):
    raw = mine[...].astype(F32) + theirs[...].astype(F32)
    factor = jnp.dot(inverse[...], raw, precision=HIGHEST, preferred_element_type=F32) * (1.0 / replicas)
    q_factor[...] = factor
    rounded = factor.astype(BF16).astype(F32)
    solved = lax.dot_general(
        inverse[...], rounded, (((0,), (0,)), ((), ())), precision=HIGHEST, preferred_element_type=F32
    )
    high = solved.astype(BF16)
    halves[...] = jnp.concatenate([high, (solved - high.astype(F32)).astype(BF16)], axis=0)
    copies = []
    for chunk in range(merged.shape[0] // STEP):
        here = rows_of(chunk)
        rebuilt = jnp.dot(turned[here, :], halves[...], preferred_element_type=F32)
        result[here, :] = (merged[here, :].astype(F32) - rebuilt).astype(BF16)
        copies.append(pltpu.make_async_copy(result.at[here, :], new_error.at[0, here, :], done.at[chunk]))
        copies[-1].start()
    for copy in copies:
        copy.wait()


def finish(mine, theirs, inverse, turned, merged, replicas):
    rows, columns = merged.shape
    rank = inverse.shape[0]
    return pl.pallas_call(
        lambda *refs: finish_kernel(replicas, *refs),
        in_specs=[WHOLE] * 5,
        out_specs=[ANYWHERE, WHOLE],
        out_shape=[
            pltpu.HBM((1, rows, columns), BF16),
            jax.ShapeDtypeStruct((rank, columns), F32),
        ],
        scratch_shapes=[
            pltpu.VMEM((2 * rank, columns), BF16),
            pltpu.VMEM((rows, columns), BF16),
            pltpu.SemaphoreType.DMA((rows // STEP,)),
        ],
        compiler_params=params(),
        cost_estimate=pl.CostEstimate(flops=4 * rank * rows * columns, bytes_accessed=4 * rows * columns, transcendentals=0),
        name="finish",
    )(in_vmem(mine), in_vmem(theirs), in_vmem(inverse), in_vmem(turned), in_vmem(merged))


def exchange(blocks, axis):
    return lax.all_to_all(blocks, axis, 0, 0, tiled=True)


def share(block, axis):
    return exchange(jnp.broadcast_to(block[None], (lax.axis_size(axis),) + block.shape), axis)


def total(blocks):
    terms = [block.astype(F32) for block in blocks]
    while len(terms) > 1:
        terms = [a + b for a, b in zip(terms[::2], terms[1::2])]
    return terms[0]


def swap(block, axis, mask):
    return lax.ppermute(block, axis, [(i, i ^ mask) for i in range(lax.axis_size(axis))])


def per_device(gradient, error, warm_start):
    replicas = lax.axis_size("rep")
    merged, part = merge(gradient, error, warm_start)
    own = total(exchange(part, "col"))
    own = total(share(own.astype(BF16), "rep"))
    p_sum = share(own.astype(BF16), "col")
    raw = raw_factor(p_sum, merged)
    inverse, turned = solve(p_sum)
    raw = total([raw] + [swap(raw, "rep", mask) for mask in (1, 2, 3)]).astype(BF16)
    return tuple(finish(raw, swap(raw, "rep", 6), inverse, turned, merged, replicas))


def solution(mesh):
    in_specs = (P("rep", None, "col"), P("rep", None, "col"), P(None, "col"))
    out_specs = (P("rep", None, "col"), P(None, "col"))
    return jax.shard_map(
        per_device, mesh=mesh, in_specs=in_specs, out_specs=out_specs, check_vma=False
    )
```

```python
import jax
import jax.numpy as jnp
from jax import lax
from jax.experimental import pallas as pl
from jax.experimental.pallas import tpu as pltpu
from jax.sharding import PartitionSpec as P

BF16, F32 = jnp.bfloat16, jnp.float32
HIGHEST = lax.Precision.HIGHEST
CORES = 2
LANES = 128
STEP = 512
WHOLE = pl.BlockSpec(memory_space=pltpu.VMEM)
ANYWHERE = pl.BlockSpec(memory_space=pl.ANY)


def params():
    return pltpu.CompilerParams(vmem_limit_bytes=40 << 20)


def in_vmem(array):
    return pltpu.with_memory_space_constraint(array, pltpu.VMEM)


def in_hbm(array):
    return pltpu.with_memory_space_constraint(array, pltpu.HBM)


def rows_of(chunk, first=0):
    return pl.ds(pl.multiple_of(first + chunk * STEP, STEP), STEP)


def core():
    return lax.rem(lax.axis_index("col"), CORES)


def merge_kernel(own, gradient, error, warm, merged, part, gradient_in, error_in, warm_in, done):
    chunks = merged.shape[0] // STEP
    first = (core() if own else 1 - core()) * merged.shape[0]
    copies = [pltpu.make_async_copy(warm, warm_in, done.at[2 * chunks])]
    for chunk in range(chunks):
        here, there = rows_of(chunk), rows_of(chunk, first)
        copies.append(pltpu.make_async_copy(gradient.at[0, there, :], gradient_in.at[here, :], done.at[2 * chunk]))
        copies.append(pltpu.make_async_copy(error.at[0, there, :], error_in.at[here, :], done.at[2 * chunk + 1]))
    for copy in copies:
        copy.start()
    copies[0].wait()
    for chunk in range(chunks):
        here = rows_of(chunk)
        copies[2 * chunk + 1].wait()
        copies[2 * chunk + 2].wait()
        value = (gradient_in[here, :].astype(F32) + error_in[here, :].astype(F32)).astype(BF16)
        merged[here, :] = value
        product = lax.dot_general(warm_in[...], value, (((1,), (1,)), ((), ())), preferred_element_type=F32)
        for block in range(STEP // LANES):
            part[chunk * (STEP // LANES) + block] = product[:, block * LANES : (block + 1) * LANES].astype(part.dtype)


def merge(gradient, error, warm, own):
    _, rows, columns = gradient.shape
    rank, half = warm.shape[0], rows // CORES
    return pl.pallas_call(
        lambda *refs: merge_kernel(own, *refs),
        in_specs=[ANYWHERE] * 3,
        out_specs=[WHOLE, WHOLE],
        out_shape=[
            pltpu.VMEM((half, columns), BF16),
            pltpu.VMEM((half // LANES, rank, LANES), F32 if own else BF16),
        ],
        scratch_shapes=[
            pltpu.VMEM((half, columns), BF16),
            pltpu.VMEM((half, columns), BF16),
            pltpu.VMEM((rank, columns), BF16),
            pltpu.SemaphoreType.DMA((2 * (half // STEP) + 1,)),
        ],
        compiler_params=params(),
        cost_estimate=pl.CostEstimate(flops=2 * rank * half * columns, bytes_accessed=4 * half * columns, transcendentals=0),
        name="merge_own" if own else "merge_other",
    )(in_hbm(gradient), in_hbm(error), in_hbm(warm))


def side_by_side(blocks):
    return jnp.concatenate([blocks[i] for i in range(blocks.shape[0])], axis=1)


def half_kernel(p_half, merged, raw):
    raw[...] = jnp.dot(side_by_side(p_half), merged[...], preferred_element_type=F32)


def rest_kernel(p_half, merged, begun, raw):
    raw[...] = (begun[...] + jnp.dot(side_by_side(p_half), merged[...], preferred_element_type=F32)).astype(BF16)


def raw_factor(p_half, merged, *begun):
    half, columns = merged.shape
    rank = p_half.shape[1]
    return pl.pallas_call(
        rest_kernel if begun else half_kernel,
        in_specs=[WHOLE] * (2 + len(begun)),
        out_specs=WHOLE,
        out_shape=pltpu.VMEM((rank, columns), BF16 if begun else F32),
        compiler_params=params(),
        cost_estimate=pl.CostEstimate(flops=2 * rank * half * columns, bytes_accessed=2 * half * columns, transcendentals=0),
        name="raw_rest" if begun else "raw_half",
    )(*(in_vmem(x) for x in (p_half, merged, *begun)))


def solve_kernel(*refs):
    *halves, inverse, turned = refs
    blocks, rank, lanes = halves[0].shape
    gram = 0.0
    for place, half in enumerate(halves):
        wide = side_by_side(half)
        gram += lax.dot_general(wide, wide, (((1,), (1,)), ((), ())), preferred_element_type=F32)
        for block in range(blocks):
            tall = half[block].astype(F32).T.astype(BF16)
            turned[pl.ds((place * blocks + block) * lanes, lanes), :] = jnp.concatenate([tall, tall], axis=1)
    row = lax.broadcasted_iota(jnp.int32, (rank, rank), 0)
    col = lax.broadcasted_iota(jnp.int32, (rank, rank), 1)
    one = (row == col).astype(F32)
    table = jnp.concatenate([gram, one], axis=1)
    below = lax.broadcasted_iota(jnp.int32, (rank, 1), 0)
    for k in range(rank):
        pivot = table[k : k + 1, :]
        factor = jnp.where(below > k, table[:, k : k + 1] / pivot[:, k : k + 1], 0.0)
        table = table - factor * pivot
    diagonal = jnp.sum(table[:, :rank] * one, axis=1, keepdims=True)
    inverse[...] = table[:, rank:] * lax.rsqrt(diagonal)


def solve(*halves):
    blocks, rank, lanes = halves[0].shape
    rows = len(halves) * blocks * lanes
    return pl.pallas_call(
        solve_kernel,
        in_specs=[WHOLE] * len(halves),
        out_specs=[WHOLE, WHOLE],
        out_shape=[pltpu.VMEM((rank, rank), F32), pltpu.VMEM((rows, 2 * rank), BF16)],
        compiler_params=params(),
        cost_estimate=pl.CostEstimate(flops=16 * rank * rank * rows, bytes_accessed=4 << 20, transcendentals=0),
        name="solve",
    )(*(in_vmem(half) for half in halves))


def finish_kernel(replicas, mine, theirs, inverse, turned, own, other, new_error, q_factor, halves, result, done):
    raw = mine[...].astype(F32) + theirs[...].astype(F32)
    factor = jnp.dot(inverse[...], raw, precision=HIGHEST, preferred_element_type=F32) * (1.0 / replicas)
    q_factor[...] = factor
    rounded = factor.astype(BF16).astype(F32)
    solved = lax.dot_general(
        inverse[...], rounded, (((0,), (0,)), ((), ())), precision=HIGHEST, preferred_element_type=F32
    )
    high = solved.astype(BF16)
    halves[...] = jnp.concatenate([high, (solved - high.astype(F32)).astype(BF16)], axis=0)
    copies = []
    half = own.shape[0]
    for merged, first, begin in ((own, core() * half, 0), (other, (1 - core()) * half, half)):
        for chunk in range(half // STEP):
            place = begin // STEP + chunk
            here = rows_of(place)
            rebuilt = jnp.dot(turned[here, :], halves[...], preferred_element_type=F32)
            result[here, :] = (merged[rows_of(chunk), :].astype(F32) - rebuilt).astype(BF16)
            copies.append(
                pltpu.make_async_copy(result.at[here, :], new_error.at[0, rows_of(chunk, first), :], done.at[place])
            )
            copies[-1].start()
    for copy in copies:
        copy.wait()


def finish(mine, theirs, inverse, turned, own, other, replicas):
    half, columns = own.shape
    rows, rank = 2 * half, inverse.shape[0]
    return pl.pallas_call(
        lambda *refs: finish_kernel(replicas, *refs),
        in_specs=[WHOLE] * 6,
        out_specs=[ANYWHERE, WHOLE],
        out_shape=[
            pltpu.HBM((1, rows, columns), BF16),
            jax.ShapeDtypeStruct((rank, columns), F32),
        ],
        scratch_shapes=[
            pltpu.VMEM((2 * rank, columns), BF16),
            pltpu.VMEM((rows, columns), BF16),
            pltpu.SemaphoreType.DMA((rows // STEP,)),
        ],
        compiler_params=params(),
        cost_estimate=pl.CostEstimate(flops=4 * rank * rows * columns, bytes_accessed=4 * rows * columns, transcendentals=0),
        name="finish",
    )(*(in_vmem(x) for x in (mine, theirs, inverse, turned, own, other)))


def exchange(blocks, axis, groups=None):
    return lax.all_to_all(blocks, axis, 0, 0, axis_index_groups=groups, tiled=True)


def share(block, axis, groups=None):
    count = len(groups[0]) if groups else lax.axis_size(axis)
    return exchange(jnp.broadcast_to(block[None], (count,) + block.shape), axis, groups)


def swap(block, axis, mask):
    return lax.ppermute(block, axis, [(i, i ^ mask) for i in range(lax.axis_size(axis))])


def total(blocks):
    terms = [block.astype(F32) for block in blocks]
    while len(terms) > 1:
        terms = [a + b for a, b in zip(terms[::2], terms[1::2])]
    return terms[0]


def per_device(gradient, error, warm_start):
    replicas = lax.axis_size("rep")
    chips = [list(range(c, lax.axis_size("col"), CORES)) for c in range(CORES)]
    other, part_other = merge(gradient, error, warm_start, own=False)
    part_other = swap(part_other, "col", 1)
    own, part = merge(gradient, error, warm_start, own=True)
    part = (part + part_other.astype(F32)).astype(BF16)
    block = total(exchange(part, "col", chips))
    block = total(share(block.astype(BF16), "rep"))
    p_own = share(block.astype(BF16), "col", chips)
    p_other = swap(p_own, "col", 1)
    raw = raw_factor(p_other, other, raw_factor(p_own, own))
    inverse, turned = solve(p_own, p_other)
    raw = total([raw] + [swap(raw, "rep", mask) for mask in (1, 2, 3)]).astype(BF16)
    return tuple(finish(raw, swap(raw, "rep", 6), inverse, turned, own, other, replicas))


def solution(mesh):
    in_specs = (P("rep", None, "col"), P("rep", None, "col"), P(None, "col"))
    out_specs = (P("rep", None, "col"), P(None, "col"))
    return jax.shard_map(
        per_device, mesh=mesh, in_specs=in_specs, out_specs=out_specs, check_vma=False
    )
```

```python
import jax
import jax.numpy as jnp
from jax import lax
from jax.experimental import pallas as pl
from jax.experimental.pallas import tpu as pltpu
from jax.sharding import PartitionSpec as P

BF16, F32 = jnp.bfloat16, jnp.float32
HIGHEST = lax.Precision.HIGHEST
CORES = 2
LANES = 128
STEP = 512
WHOLE = pl.BlockSpec(memory_space=pltpu.VMEM)
ANYWHERE = pl.BlockSpec(memory_space=pl.ANY)


def params():
    return pltpu.CompilerParams(vmem_limit_bytes=40 << 20)


def in_vmem(array):
    return pltpu.with_memory_space_constraint(array, pltpu.VMEM)


def in_hbm(array):
    return pltpu.with_memory_space_constraint(array, pltpu.HBM)


def rows_of(chunk, first=0):
    return pl.ds(pl.multiple_of(first + chunk * STEP, STEP), STEP)


def core():
    return lax.rem(lax.axis_index("col"), CORES)


def merge_chunks(steps, gradient, error, warm, merged, columns_in, warm_in, done):
    copies = [pltpu.make_async_copy(warm, warm_in, done.at[2 * len(steps)])]
    for place, (chunk, first, _) in enumerate(steps):
        there = rows_of(chunk, first)
        copies.append(pltpu.make_async_copy(gradient.at[0, there, :], columns_in.at[2 * place], done.at[2 * place]))
        copies.append(pltpu.make_async_copy(error.at[0, there, :], columns_in.at[2 * place + 1], done.at[2 * place + 1]))
    for copy in copies:
        copy.start()
    copies[0].wait()
    for place, (chunk, first, blocks) in enumerate(steps):
        copies[2 * place + 1].wait()
        copies[2 * place + 2].wait()
        value = (columns_in[2 * place].astype(F32) + columns_in[2 * place + 1].astype(F32)).astype(BF16)
        merged[rows_of(chunk, first), :] = value
        product = lax.dot_general(warm_in[...], value, (((1,), (1,)), ((), ())), preferred_element_type=F32)
        for block in range(STEP // LANES):
            blocks[chunk * (STEP // LANES) + block] = product[:, block * LANES : (block + 1) * LANES].astype(blocks.dtype)


def begin_kernel(early, gradient, error, warm, merged, part_own, part_other, *scratch):
    half = merged.shape[0] // CORES
    own, other = core() * half, (1 - core()) * half
    steps = [(chunk, other, part_other) for chunk in range(half // STEP)]
    steps += [(chunk, own, part_own) for chunk in range(early)]
    merge_chunks(steps, gradient, error, warm, merged, *scratch)


def end_kernel(early, gradient, error, warm, merged_in, part_in, merged, part_own, *scratch):
    half = merged.shape[0] // CORES
    steps = [(chunk, core() * half, part_own) for chunk in range(early, half // STEP)]
    merge_chunks(steps, gradient, error, warm, merged, *scratch)


def merge_call(kernel, early, chunks, arrays, begun, out_shape, name):
    _, _, columns = arrays[0].shape
    rank = arrays[2].shape[0]
    rows = chunks * STEP
    return pl.pallas_call(
        lambda *refs: kernel(early, *refs),
        in_specs=[ANYWHERE] * len(arrays) + [WHOLE] * len(begun),
        out_specs=[WHOLE] * len(out_shape),
        out_shape=out_shape,
        input_output_aliases={len(arrays) + i: i for i in range(len(begun))},
        scratch_shapes=[
            pltpu.VMEM((2 * chunks, STEP, columns), BF16),
            pltpu.VMEM((rank, columns), BF16),
            pltpu.SemaphoreType.DMA((2 * chunks + 1,)),
        ],
        compiler_params=params(),
        cost_estimate=pl.CostEstimate(flops=2 * rank * rows * columns, bytes_accessed=4 * rows * columns, transcendentals=0),
        name=name,
    )(*(in_hbm(x) for x in arrays), *(in_vmem(x) for x in begun))


def merge(gradient, error, warm):
    arrays = (gradient, error, warm)
    _, rows, columns = gradient.shape
    blocks = (rows // CORES // LANES, warm.shape[0], LANES)
    chunks = rows // STEP
    late = chunks // 4
    shapes = [pltpu.VMEM((rows, columns), BF16), pltpu.VMEM(blocks, F32), pltpu.VMEM(blocks, BF16)]
    early = chunks // CORES - late
    *begun, part_other = merge_call(begin_kernel, early, chunks - late, arrays, (), shapes, "merge_begin")
    part_other = swap(part_other, "col", 1)
    merged, part = merge_call(end_kernel, early, late, arrays, begun, shapes[:2], "merge_end")
    return merged, (part + part_other.astype(F32)).astype(BF16)


def side_by_side(p_sum):
    blocks = p_sum.shape[0]
    chips = blocks // CORES
    return jnp.concatenate([p_sum[i % chips * CORES + i // chips] for i in range(blocks)], axis=1)


def raw_kernel(p_sum, merged, raw):
    raw[...] = jnp.dot(side_by_side(p_sum), merged[...], preferred_element_type=F32).astype(BF16)


def raw_factor(p_sum, merged):
    rows, columns = merged.shape
    rank = p_sum.shape[1]
    return pl.pallas_call(
        raw_kernel,
        in_specs=[WHOLE, WHOLE],
        out_specs=WHOLE,
        out_shape=pltpu.VMEM((rank, columns), BF16),
        compiler_params=params(),
        cost_estimate=pl.CostEstimate(flops=2 * rank * rows * columns, bytes_accessed=2 * rows * columns, transcendentals=0),
        name="raw_factor",
    )(in_vmem(p_sum), in_vmem(merged))


def turn_kernel(p_sum, gram, turned):
    blocks, rank, lanes = p_sum.shape
    wide = side_by_side(p_sum)
    gram[...] = lax.dot_general(wide, wide, (((1,), (1,)), ((), ())), preferred_element_type=F32)
    for block in range(blocks):
        tall = wide[:, block * lanes : (block + 1) * lanes].astype(F32).T.astype(BF16)
        turned[pl.ds(block * lanes, lanes), :] = jnp.concatenate([tall, tall], axis=1)


def turn(p_sum):
    blocks, rank, lanes = p_sum.shape
    return pl.pallas_call(
        turn_kernel,
        in_specs=[WHOLE],
        out_specs=[WHOLE, WHOLE],
        out_shape=[pltpu.VMEM((rank, rank), F32), pltpu.VMEM((blocks * lanes, 2 * rank), BF16)],
        compiler_params=params(),
        cost_estimate=pl.CostEstimate(flops=8 * rank * rank * blocks * lanes, bytes_accessed=2 << 20, transcendentals=0),
        name="turn",
    )(in_vmem(p_sum))


def solve_kernel(gram, inverse):
    rank = gram.shape[0]
    row = lax.broadcasted_iota(jnp.int32, (rank, rank), 0)
    col = lax.broadcasted_iota(jnp.int32, (rank, rank), 1)
    one = (row == col).astype(F32)
    table = jnp.concatenate([gram[...], one], axis=1)
    below = lax.broadcasted_iota(jnp.int32, (rank, 1), 0)
    for k in range(rank):
        pivot = table[k : k + 1, :]
        factor = jnp.where(below > k, table[:, k : k + 1] / pivot[:, k : k + 1], 0.0)
        table = table - factor * pivot
    diagonal = jnp.sum(table[:, :rank] * one, axis=1, keepdims=True)
    inverse[...] = table[:, rank:] * lax.rsqrt(diagonal)


def solve(gram):
    return pl.pallas_call(
        solve_kernel,
        in_specs=[WHOLE],
        out_specs=WHOLE,
        out_shape=pltpu.VMEM(gram.shape, F32),
        compiler_params=params(),
        cost_estimate=pl.CostEstimate(flops=8 << 20, bytes_accessed=4 << 20, transcendentals=0),
        name="solve",
    )(in_vmem(gram))


def finish_kernel(replicas, mine, theirs, inverse, turned, merged, new_error, q_factor, halves, result, done):
    raw = mine[...].astype(F32) + theirs[...].astype(F32)
    factor = jnp.dot(inverse[...], raw, precision=HIGHEST, preferred_element_type=F32) * (1.0 / replicas)
    q_factor[...] = factor
    rounded = factor.astype(BF16).astype(F32)
    solved = lax.dot_general(
        inverse[...], rounded, (((0,), (0,)), ((), ())), precision=HIGHEST, preferred_element_type=F32
    )
    high = solved.astype(BF16)
    halves[...] = jnp.concatenate([high, (solved - high.astype(F32)).astype(BF16)], axis=0)
    copies = []
    for chunk in range(merged.shape[0] // STEP):
        here = rows_of(chunk)
        rebuilt = jnp.dot(turned[here, :], halves[...], preferred_element_type=F32)
        result[here, :] = (merged[here, :].astype(F32) - rebuilt).astype(BF16)
        copies.append(pltpu.make_async_copy(result.at[here, :], new_error.at[0, here, :], done.at[chunk]))
        copies[-1].start()
    for copy in copies:
        copy.wait()


def finish(mine, theirs, inverse, turned, merged, replicas):
    rows, columns = merged.shape
    rank = inverse.shape[0]
    return pl.pallas_call(
        lambda *refs: finish_kernel(replicas, *refs),
        in_specs=[WHOLE] * 5,
        out_specs=[ANYWHERE, WHOLE],
        out_shape=[
            pltpu.HBM((1, rows, columns), BF16),
            jax.ShapeDtypeStruct((rank, columns), F32),
        ],
        scratch_shapes=[
            pltpu.VMEM((2 * rank, columns), BF16),
            pltpu.VMEM((rows, columns), BF16),
            pltpu.SemaphoreType.DMA((rows // STEP,)),
        ],
        compiler_params=params(),
        cost_estimate=pl.CostEstimate(flops=4 * rank * rows * columns, bytes_accessed=4 * rows * columns, transcendentals=0),
        name="finish",
    )(in_vmem(mine), in_vmem(theirs), in_vmem(inverse), in_vmem(turned), in_vmem(merged))


def exchange(blocks, axis, groups=None):
    return lax.all_to_all(blocks, axis, 0, 0, axis_index_groups=groups, tiled=True)


def share(block, axis):
    return exchange(jnp.broadcast_to(block[None], (lax.axis_size(axis),) + block.shape), axis)


def swap(block, axis, mask):
    return lax.ppermute(block, axis, [(i, i ^ mask) for i in range(lax.axis_size(axis))])


def total(blocks):
    terms = [block.astype(F32) for block in blocks]
    while len(terms) > 1:
        terms = [a + b for a, b in zip(terms[::2], terms[1::2])]
    return terms[0]


def per_device(gradient, error, warm_start):
    replicas = lax.axis_size("rep")
    chips = [list(range(c, lax.axis_size("col"), CORES)) for c in range(CORES)]
    merged, part = merge(gradient, error, warm_start)
    own = total(exchange(part, "col", chips))
    own = total(share(own.astype(BF16), "rep"))
    p_sum = share(own.astype(BF16), "col")
    raw = raw_factor(p_sum, merged)
    gram, turned = turn(p_sum)
    near = [swap(raw, "rep", mask) for mask in (1, 2, 3)]
    raw, gram, *near = lax.optimization_barrier((raw, gram, *near))
    raw = total([raw, *near]).astype(BF16)
    inverse = solve(gram)
    return tuple(finish(raw, swap(raw, "rep", 6), inverse, turned, merged, replicas))


def solution(mesh):
    in_specs = (P("rep", None, "col"), P("rep", None, "col"), P(None, "col"))
    out_specs = (P("rep", None, "col"), P(None, "col"))
    return jax.shard_map(
        per_device, mesh=mesh, in_specs=in_specs, out_specs=out_specs, check_vma=False
    )
```

```python
import jax
import jax.numpy as jnp
from jax import lax
from jax.experimental import pallas as pl
from jax.experimental.pallas import tpu as pltpu
from jax.sharding import PartitionSpec as P

BF16, F32 = jnp.bfloat16, jnp.float32
HIGHEST = lax.Precision.HIGHEST
CORES = 2
LANES = 128
STEP = 512
WHOLE = pl.BlockSpec(memory_space=pltpu.VMEM)
ANYWHERE = pl.BlockSpec(memory_space=pl.ANY)


def params():
    return pltpu.CompilerParams(vmem_limit_bytes=32 << 20)


def in_vmem(array):
    return pltpu.with_memory_space_constraint(array, pltpu.VMEM)


def in_hbm(array):
    return pltpu.with_memory_space_constraint(array, pltpu.HBM)


def rows_of(chunk):
    return pl.ds(chunk * STEP, STEP)


def merge_kernel(gradient, error, warm, merged, part, gradient_in, error_in, warm_in, done):
    chunks = merged.shape[0] // STEP
    copies = [pltpu.make_async_copy(warm, warm_in, done.at[2 * chunks])]
    for chunk in range(chunks):
        here = rows_of(chunk)
        copies.append(pltpu.make_async_copy(gradient.at[0, here, :], gradient_in.at[here, :], done.at[2 * chunk]))
        copies.append(pltpu.make_async_copy(error.at[0, here, :], error_in.at[here, :], done.at[2 * chunk + 1]))
    for copy in copies:
        copy.start()
    copies[0].wait()
    for chunk in range(chunks):
        here = rows_of(chunk)
        copies[2 * chunk + 1].wait()
        copies[2 * chunk + 2].wait()
        value = (gradient_in[here, :].astype(F32) + error_in[here, :].astype(F32)).astype(BF16)
        merged[here, :] = value
        product = lax.dot_general(warm_in[...], value, (((1,), (1,)), ((), ())), preferred_element_type=F32)
        for block in range(STEP // LANES):
            part[chunk * (STEP // LANES) + block] = product[:, block * LANES : (block + 1) * LANES].astype(BF16)


def merge(gradient, error, warm):
    _, rows, columns = gradient.shape
    rank = warm.shape[0]
    return pl.pallas_call(
        merge_kernel,
        in_specs=[ANYWHERE] * 3,
        out_specs=[WHOLE, WHOLE],
        out_shape=[
            pltpu.VMEM((rows, columns), BF16),
            pltpu.VMEM((rows // LANES, rank, LANES), BF16),
        ],
        scratch_shapes=[
            pltpu.VMEM((rows, columns), BF16),
            pltpu.VMEM((rows, columns), BF16),
            pltpu.VMEM((rank, columns), BF16),
            pltpu.SemaphoreType.DMA((2 * (rows // STEP) + 1,)),
        ],
        compiler_params=params(),
        cost_estimate=pl.CostEstimate(flops=2 * rank * rows * columns, bytes_accessed=4 * rows * columns, transcendentals=0),
        name="merge",
    )(in_hbm(gradient), in_hbm(error), in_hbm(warm))


def side_by_side(blocks):
    return jnp.concatenate([blocks[i] for i in range(blocks.shape[0])], axis=1)


def leads():
    return lax.rem(lax.axis_index("col"), CORES) == 1


def raw_kernel(p_sum, own, other, raw):
    @pl.when(leads())
    def _():
        wide = side_by_side(p_sum)
        for place, merged in enumerate((own, other)):
            raw[place] = jnp.dot(wide, merged[...], preferred_element_type=F32).astype(BF16)

    @pl.when(jnp.logical_not(leads()))
    def _():
        raw[...] = jnp.zeros_like(raw)


def raw_factors(p_sum, own, other):
    rows, columns = own.shape
    rank = p_sum.shape[1]
    return pl.pallas_call(
        raw_kernel,
        in_specs=[WHOLE] * 3,
        out_specs=WHOLE,
        out_shape=pltpu.VMEM((CORES, rank, columns), BF16),
        compiler_params=params(),
        cost_estimate=pl.CostEstimate(flops=4 * rank * rows * columns, bytes_accessed=4 * rows * columns, transcendentals=0),
        name="raw_factors",
    )(in_vmem(p_sum), in_vmem(own), in_vmem(other))


def solve_kernel(p_sum, inverse, turned):
    blocks, rank, lanes = p_sum.shape
    wide = side_by_side(p_sum)
    gram = lax.dot_general(wide, wide, (((1,), (1,)), ((), ())), preferred_element_type=F32)
    for block in range(blocks):
        tall = p_sum[block].astype(F32).T.astype(BF16)
        turned[pl.ds(block * lanes, lanes), :] = jnp.concatenate([tall, tall], axis=1)
    row = lax.broadcasted_iota(jnp.int32, (rank, rank), 0)
    col = lax.broadcasted_iota(jnp.int32, (rank, rank), 1)
    one = (row == col).astype(F32)
    table = jnp.concatenate([gram, one], axis=1)
    below = lax.broadcasted_iota(jnp.int32, (rank, 1), 0)
    for k in range(rank):
        pivot = table[k : k + 1, :]
        factor = jnp.where(below > k, table[:, k : k + 1] / pivot[:, k : k + 1], 0.0)
        table = table - factor * pivot
    diagonal = jnp.sum(table[:, :rank] * one, axis=1, keepdims=True)
    inverse[...] = table[:, rank:] * lax.rsqrt(diagonal)


def solve(p_sum):
    blocks, rank, lanes = p_sum.shape
    return pl.pallas_call(
        solve_kernel,
        in_specs=[WHOLE],
        out_specs=[WHOLE, WHOLE],
        out_shape=[pltpu.VMEM((rank, rank), F32), pltpu.VMEM((blocks * lanes, 2 * rank), BF16)],
        compiler_params=params(),
        cost_estimate=pl.CostEstimate(flops=16 * rank * rank * blocks * lanes, bytes_accessed=4 << 20, transcendentals=0),
        name="solve",
    )(in_vmem(p_sum))


def finish_rows(replicas, raw, inverse, turned, merged, new_error, q_factor, halves, result, done):
    factor = jnp.dot(inverse[...], raw[...], precision=HIGHEST, preferred_element_type=F32) * (1.0 / replicas)
    q_factor[...] = factor
    rounded = factor.astype(BF16).astype(F32)
    solved = lax.dot_general(
        inverse[...], rounded, (((0,), (0,)), ((), ())), precision=HIGHEST, preferred_element_type=F32
    )
    high = solved.astype(BF16)
    halves[...] = jnp.concatenate([high, (solved - high.astype(F32)).astype(BF16)], axis=0)
    copies = []
    for chunk in range(merged.shape[0] // STEP):
        here = rows_of(chunk)
        rebuilt = jnp.dot(turned[here, :], halves[...], preferred_element_type=F32)
        result[here, :] = (merged[here, :].astype(F32) - rebuilt).astype(BF16)
        copies.append(pltpu.make_async_copy(result.at[here, :], new_error.at[0, here, :], done.at[chunk]))
        copies[-1].start()
    for copy in copies:
        copy.wait()


def first_kernel(replicas, raw, inverse, turned, merged, new_error, q_factor, *scratch):
    @pl.when(leads())
    def _():
        finish_rows(replicas, raw, inverse, turned, merged, new_error, q_factor, *scratch)

    @pl.when(jnp.logical_not(leads()))
    def _():
        q_factor[...] = jnp.zeros_like(q_factor)


def second_kernel(replicas, raw, inverse, turned, merged, _, q_begun, new_error, q_factor, *scratch):
    @pl.when(leads())
    def _():
        q_factor[...] = q_begun[...]

    @pl.when(jnp.logical_not(leads()))
    def _():
        finish_rows(replicas, raw, inverse, turned, merged, new_error, q_factor, *scratch)


def finish(raw, inverse, turned, merged, replicas, *begun):
    rows, columns = merged.shape
    rank = inverse.shape[0]
    kernel = second_kernel if begun else first_kernel
    return pl.pallas_call(
        lambda *refs: kernel(replicas, *refs),
        in_specs=[WHOLE] * 4 + [ANYWHERE, WHOLE][: len(begun)],
        out_specs=[ANYWHERE, WHOLE],
        out_shape=[
            pltpu.HBM((1, rows, columns), BF16),
            jax.ShapeDtypeStruct((rank, columns), F32),
        ],
        input_output_aliases={4: 0} if begun else {},
        scratch_shapes=[
            pltpu.VMEM((2 * rank, columns), BF16),
            pltpu.VMEM((rows, columns), BF16),
            pltpu.SemaphoreType.DMA((rows // STEP,)),
        ],
        compiler_params=params(),
        cost_estimate=pl.CostEstimate(flops=4 * rank * rows * columns, bytes_accessed=4 * rows * columns, transcendentals=0),
        name="finish_other" if begun else "finish_leading",
    )(*(in_vmem(x) for x in (raw, inverse, turned, merged)), *begun)


def exchange(blocks, axis, groups=None):
    return lax.all_to_all(blocks, axis, 0, 0, axis_index_groups=groups, tiled=True)


def share(block, axis, groups=None):
    count = len(groups[0]) if groups else lax.axis_size(axis)
    return exchange(jnp.broadcast_to(block[None], (count,) + block.shape), axis, groups)


def swap_cores(block):
    return lax.ppermute(block, "col", [(i, i ^ 1) for i in range(lax.axis_size("col"))])


def swap_chips(block, mask, idle):
    columns, replicas = lax.axis_size("col"), lax.axis_size("rep")
    pairs = []
    for c in range(columns):
        for r in range(replicas):
            partner = (c, r ^ mask) if c % CORES else (c ^ idle[0], r ^ idle[1])
            pairs.append((c * replicas + r, partner[0] * replicas + partner[1]))
    return lax.ppermute(block, ("col", "rep"), pairs)


def total(blocks):
    terms = [block.astype(F32) for block in blocks]
    while len(terms) > 1:
        terms = [a + b for a, b in zip(terms[::2], terms[1::2])]
    return terms[0]


def left_factor(part):
    chips = [list(range(c, lax.axis_size("col"), CORES)) for c in range(CORES)]
    count = len(chips[0])
    blocks = exchange(part, "col", chips)
    own = total(blocks.reshape((count, -1) + blocks.shape[1:])).astype(BF16)
    own = total(share(own, "rep")).astype(BF16)
    return share(own, "col", chips).reshape(part.shape)


def per_device(gradient, error, warm_start):
    replicas = lax.axis_size("rep")
    merged, part = merge(gradient, error, warm_start)
    handed, merged = lax.optimization_barrier((swap_cores(part), merged))
    part = total([part, handed]).astype(BF16)
    other = swap_cores(merged)
    p_sum = left_factor(part)
    raw = raw_factors(p_sum, merged, other)
    inverse, turned = solve(p_sum)
    near = [swap_chips(raw, 1, (0, 1)), swap_chips(raw, 2, (8, 0)), swap_chips(raw, 3, (2, 0))]
    raw, inverse, *near = lax.optimization_barrier((raw, inverse, *near))
    raw = total([raw, *near]).astype(BF16)
    raw = total([raw, swap_chips(raw, 6, (0, 1))])
    begun = finish(raw[0], inverse, turned, merged, replicas)
    return tuple(finish(swap_cores(raw[1]), inverse, turned, merged, replicas, *begun))


def solution(mesh):
    in_specs = (P("rep", None, "col"), P("rep", None, "col"), P(None, "col"))
    out_specs = (P("rep", None, "col"), P(None, "col"))
    return jax.shard_map(
        per_device, mesh=mesh, in_specs=in_specs, out_specs=out_specs, check_vma=False
    )
```

```python
import jax
import jax.numpy as jnp
from jax import lax
from jax.experimental import pallas as pl
from jax.experimental.pallas import tpu as pltpu
from jax.sharding import PartitionSpec as P

BF16, F32 = jnp.bfloat16, jnp.float32
HIGHEST = lax.Precision.HIGHEST
CORES = 2
LANES = 128
STEP = 512
WHOLE = pl.BlockSpec(memory_space=pltpu.VMEM)
ANYWHERE = pl.BlockSpec(memory_space=pl.ANY)


def params():
    return pltpu.CompilerParams(vmem_limit_bytes=32 << 20)


def in_vmem(array):
    return pltpu.with_memory_space_constraint(array, pltpu.VMEM)


def in_hbm(array):
    return pltpu.with_memory_space_constraint(array, pltpu.HBM)


def rows_of(chunk):
    return pl.ds(chunk * STEP, STEP)


def merge_kernel(gradient, error, warm, merged, part, gradient_in, error_in, warm_in, done):
    chunks = merged.shape[0] // STEP
    copies = [pltpu.make_async_copy(warm, warm_in, done.at[2 * chunks])]
    for chunk in range(chunks):
        here = rows_of(chunk)
        copies.append(pltpu.make_async_copy(gradient.at[0, here, :], gradient_in.at[here, :], done.at[2 * chunk]))
        copies.append(pltpu.make_async_copy(error.at[0, here, :], error_in.at[here, :], done.at[2 * chunk + 1]))
    for copy in copies:
        copy.start()
    copies[0].wait()
    for chunk in range(chunks):
        here = rows_of(chunk)
        copies[2 * chunk + 1].wait()
        copies[2 * chunk + 2].wait()
        value = (gradient_in[here, :].astype(F32) + error_in[here, :].astype(F32)).astype(BF16)
        merged[here, :] = value
        product = lax.dot_general(warm_in[...], value, (((1,), (1,)), ((), ())), preferred_element_type=F32)
        for block in range(STEP // LANES):
            part[chunk * (STEP // LANES) + block] = product[:, block * LANES : (block + 1) * LANES].astype(BF16)


def merge(gradient, error, warm):
    _, rows, columns = gradient.shape
    rank = warm.shape[0]
    return pl.pallas_call(
        merge_kernel,
        in_specs=[ANYWHERE] * 3,
        out_specs=[WHOLE, WHOLE],
        out_shape=[
            pltpu.VMEM((rows, columns), BF16),
            pltpu.VMEM((rows // LANES, rank, LANES), BF16),
        ],
        scratch_shapes=[
            pltpu.VMEM((rows, columns), BF16),
            pltpu.VMEM((rows, columns), BF16),
            pltpu.VMEM((rank, columns), BF16),
            pltpu.SemaphoreType.DMA((2 * (rows // STEP) + 1,)),
        ],
        compiler_params=params(),
        cost_estimate=pl.CostEstimate(flops=2 * rank * rows * columns, bytes_accessed=4 * rows * columns, transcendentals=0),
        name="merge",
    )(in_hbm(gradient), in_hbm(error), in_hbm(warm))


def side_by_side(blocks):
    return jnp.concatenate([blocks[i] for i in range(blocks.shape[0])], axis=1)


def leads():
    return lax.rem(lax.axis_index("col"), CORES) == 1


def raw_kernel(p_sum, own, other, raw):
    @pl.when(leads())
    def _():
        wide = side_by_side(p_sum)
        for place, merged in enumerate((own, other)):
            raw[place] = jnp.dot(wide, merged[...], preferred_element_type=F32).astype(BF16)

    @pl.when(jnp.logical_not(leads()))
    def _():
        raw[...] = jnp.zeros_like(raw)


def raw_factors(p_sum, own, other):
    rows, columns = own.shape
    rank = p_sum.shape[1]
    return pl.pallas_call(
        raw_kernel,
        in_specs=[WHOLE] * 3,
        out_specs=WHOLE,
        out_shape=pltpu.VMEM((CORES, rank, columns), BF16),
        compiler_params=params(),
        cost_estimate=pl.CostEstimate(flops=4 * rank * rows * columns, bytes_accessed=4 * rows * columns, transcendentals=0),
        name="raw_factors",
    )(in_vmem(p_sum), in_vmem(own), in_vmem(other))


def turn_kernel(p_sum, gram, turned):
    blocks, rank, lanes = p_sum.shape
    wide = side_by_side(p_sum)
    gram[...] = lax.dot_general(wide, wide, (((1,), (1,)), ((), ())), preferred_element_type=F32)
    for block in range(blocks):
        tall = wide[:, block * lanes : (block + 1) * lanes].astype(F32).T.astype(BF16)
        turned[pl.ds(block * lanes, lanes), :] = jnp.concatenate([tall, tall], axis=1)


def turn(p_sum):
    blocks, rank, lanes = p_sum.shape
    return pl.pallas_call(
        turn_kernel,
        in_specs=[WHOLE],
        out_specs=[WHOLE, WHOLE],
        out_shape=[pltpu.VMEM((rank, rank), F32), pltpu.VMEM((blocks * lanes, 2 * rank), BF16)],
        compiler_params=params(),
        cost_estimate=pl.CostEstimate(flops=8 * rank * rank * blocks * lanes, bytes_accessed=2 << 20, transcendentals=0),
        name="turn",
    )(in_vmem(p_sum))


def solve_kernel(gram, inverse):
    rank = gram.shape[0]
    row = lax.broadcasted_iota(jnp.int32, (rank, rank), 0)
    col = lax.broadcasted_iota(jnp.int32, (rank, rank), 1)
    one = (row == col).astype(F32)
    table = jnp.concatenate([gram[...], one], axis=1)
    below = lax.broadcasted_iota(jnp.int32, (rank, 1), 0)
    for k in range(rank):
        pivot = table[k : k + 1, :]
        factor = jnp.where(below > k, table[:, k : k + 1] / pivot[:, k : k + 1], 0.0)
        table = table - factor * pivot
    diagonal = jnp.sum(table[:, :rank] * one, axis=1, keepdims=True)
    inverse[...] = table[:, rank:] * lax.rsqrt(diagonal)


def solve(gram):
    return pl.pallas_call(
        solve_kernel,
        in_specs=[WHOLE],
        out_specs=WHOLE,
        out_shape=pltpu.VMEM(gram.shape, F32),
        compiler_params=params(),
        cost_estimate=pl.CostEstimate(flops=8 << 20, bytes_accessed=4 << 20, transcendentals=0),
        name="solve",
    )(in_vmem(gram))


def finish_rows(replicas, raw, inverse, turned, merged, new_error, q_factor, halves, result, factor_out, done):
    factor = jnp.dot(inverse[...], raw[...], precision=HIGHEST, preferred_element_type=F32) * (1.0 / replicas)
    factor_out[...] = factor
    copies = [pltpu.make_async_copy(factor_out, q_factor, done.at[merged.shape[0] // STEP])]
    copies[0].start()
    rounded = factor.astype(BF16).astype(F32)
    solved = lax.dot_general(
        inverse[...], rounded, (((0,), (0,)), ((), ())), precision=HIGHEST, preferred_element_type=F32
    )
    high = solved.astype(BF16)
    halves[...] = jnp.concatenate([high, (solved - high.astype(F32)).astype(BF16)], axis=0)
    for chunk in range(merged.shape[0] // STEP):
        here = rows_of(chunk)
        rebuilt = jnp.dot(turned[here, :], halves[...], preferred_element_type=F32)
        result[here, :] = (merged[here, :].astype(F32) - rebuilt).astype(BF16)
        copies.append(pltpu.make_async_copy(result.at[here, :], new_error.at[0, here, :], done.at[chunk]))
        copies[-1].start()
    for copy in copies:
        copy.wait()


def first_kernel(replicas, *refs):
    @pl.when(leads())
    def _():
        finish_rows(replicas, *refs)


def second_kernel(replicas, raw, inverse, turned, merged, new_error_in, q_factor_in, *refs):
    @pl.when(jnp.logical_not(leads()))
    def _():
        finish_rows(replicas, raw, inverse, turned, merged, *refs)


def finish(raw, inverse, turned, merged, replicas, *begun):
    rows, columns = merged.shape
    rank = inverse.shape[0]
    kernel = second_kernel if begun else first_kernel
    return pl.pallas_call(
        lambda *refs: kernel(replicas, *refs),
        in_specs=[WHOLE] * 4 + [ANYWHERE] * len(begun),
        out_specs=[ANYWHERE] * 2,
        out_shape=[pltpu.HBM((1, rows, columns), BF16), pltpu.HBM((rank, columns), F32)],
        input_output_aliases={4 + i: i for i in range(len(begun))},
        scratch_shapes=[
            pltpu.VMEM((2 * rank, columns), BF16),
            pltpu.VMEM((rows, columns), BF16),
            pltpu.VMEM((rank, columns), F32),
            pltpu.SemaphoreType.DMA((rows // STEP + 1,)),
        ],
        compiler_params=params(),
        cost_estimate=pl.CostEstimate(flops=4 * rank * rows * columns, bytes_accessed=4 * rows * columns, transcendentals=0),
        name="finish_other" if begun else "finish_leading",
    )(*(in_vmem(x) for x in (raw, inverse, turned, merged)), *(in_hbm(x) for x in begun))


def exchange(blocks, axis, groups=None):
    return lax.all_to_all(blocks, axis, 0, 0, axis_index_groups=groups, tiled=True)


def share(block, axis, groups=None):
    count = len(groups[0]) if groups else lax.axis_size(axis)
    return exchange(jnp.broadcast_to(block[None], (count,) + block.shape), axis, groups)


def swap_cores(block):
    return lax.ppermute(block, "col", [(i, i ^ 1) for i in range(lax.axis_size("col"))])


def swap_chips(block, mask, idle):
    columns, replicas = lax.axis_size("col"), lax.axis_size("rep")
    pairs = []
    for c in range(columns):
        for r in range(replicas):
            partner = (c, r ^ mask) if c % CORES else (c ^ idle[0], r ^ idle[1])
            pairs.append((c * replicas + r, partner[0] * replicas + partner[1]))
    return lax.ppermute(block, ("col", "rep"), pairs)


def total(blocks):
    terms = [block.astype(F32) for block in blocks]
    while len(terms) > 1:
        terms = [a + b for a, b in zip(terms[::2], terms[1::2])]
    return terms[0]


def left_factor(part):
    chips = [list(range(c, lax.axis_size("col"), CORES)) for c in range(CORES)]
    count = len(chips[0])
    blocks = exchange(part, "col", chips)
    own = total(blocks.reshape((count, -1) + blocks.shape[1:])).astype(BF16)
    own = total(share(own, "rep")).astype(BF16)
    return share(own, "col", chips).reshape(part.shape)


def per_device(gradient, error, warm_start):
    replicas = lax.axis_size("rep")
    merged, part = merge(gradient, error, warm_start)
    handed, merged = lax.optimization_barrier((swap_cores(part), merged))
    part = total([part, handed]).astype(BF16)
    other = swap_cores(merged)
    p_sum = left_factor(part)
    raw = raw_factors(p_sum, merged, other)
    gram, turned = turn(p_sum)
    near = [swap_chips(raw, 1, (0, 1)), swap_chips(raw, 2, (8, 0)), swap_chips(raw, 3, (2, 0))]
    raw, gram, *near = lax.optimization_barrier((raw, gram, *near))
    raw = total([raw, *near]).astype(BF16)
    far, inverse = lax.optimization_barrier((swap_chips(raw, 6, (0, 1)), solve(gram)))
    raw = total([raw, far])
    begun = finish(raw[0], inverse, turned, merged, replicas)
    return tuple(finish(swap_cores(raw[1]), inverse, turned, merged, replicas, *begun))


def solution(mesh):
    in_specs = (P("rep", None, "col"), P("rep", None, "col"), P(None, "col"))
    out_specs = (P("rep", None, "col"), P(None, "col"))
    return jax.shard_map(
        per_device, mesh=mesh, in_specs=in_specs, out_specs=out_specs, check_vma=False
    )
```

```python
import jax
import jax.numpy as jnp
from jax import lax
from jax.experimental import pallas as pl
from jax.experimental.pallas import tpu as pltpu
from jax.sharding import PartitionSpec as P

BF16, F32 = jnp.bfloat16, jnp.float32
HIGHEST = lax.Precision.HIGHEST
CORES = 2
LANES = 128
STEP = 512
WHOLE = pl.BlockSpec(memory_space=pltpu.VMEM)
ANYWHERE = pl.BlockSpec(memory_space=pl.ANY)


def params():
    return pltpu.CompilerParams(vmem_limit_bytes=32 << 20)


def in_vmem(array):
    return pltpu.with_memory_space_constraint(array, pltpu.VMEM)


def in_hbm(array):
    return pltpu.with_memory_space_constraint(array, pltpu.HBM)


def rows_of(chunk):
    return pl.ds(chunk * STEP, STEP)


def merge_kernel(gradient, error, warm, merged, part, gradient_in, error_in, warm_in, done):
    chunks = merged.shape[0] // STEP
    copies = [pltpu.make_async_copy(warm, warm_in, done.at[2 * chunks])]
    for chunk in range(chunks):
        here = rows_of(chunk)
        copies.append(pltpu.make_async_copy(gradient.at[0, here, :], gradient_in.at[here, :], done.at[2 * chunk]))
        copies.append(pltpu.make_async_copy(error.at[0, here, :], error_in.at[here, :], done.at[2 * chunk + 1]))
    for copy in copies:
        copy.start()
    copies[0].wait()
    for chunk in range(chunks):
        here = rows_of(chunk)
        copies[2 * chunk + 1].wait()
        copies[2 * chunk + 2].wait()
        value = (gradient_in[here, :].astype(F32) + error_in[here, :].astype(F32)).astype(BF16)
        merged[here, :] = value
        product = lax.dot_general(warm_in[...], value, (((1,), (1,)), ((), ())), preferred_element_type=F32)
        for block in range(STEP // LANES):
            part[chunk * (STEP // LANES) + block] = product[:, block * LANES : (block + 1) * LANES].astype(BF16)


def merge(gradient, error, warm):
    _, rows, columns = gradient.shape
    rank = warm.shape[0]
    return pl.pallas_call(
        merge_kernel,
        in_specs=[ANYWHERE] * 3,
        out_specs=[WHOLE, WHOLE],
        out_shape=[
            pltpu.VMEM((rows, columns), BF16),
            pltpu.VMEM((rows // LANES, rank, LANES), BF16),
        ],
        scratch_shapes=[
            pltpu.VMEM((rows, columns), BF16),
            pltpu.VMEM((rows, columns), BF16),
            pltpu.VMEM((rank, columns), BF16),
            pltpu.SemaphoreType.DMA((2 * (rows // STEP) + 1,)),
        ],
        compiler_params=params(),
        cost_estimate=pl.CostEstimate(flops=2 * rank * rows * columns, bytes_accessed=4 * rows * columns, transcendentals=0),
        name="merge",
    )(in_hbm(gradient), in_hbm(error), in_hbm(warm))


def side_by_side(blocks):
    return jnp.concatenate([blocks[i] for i in range(blocks.shape[0])], axis=1)


def leads():
    return lax.rem(lax.axis_index("col"), CORES) == 1


def raw_kernel(p_sum, own, other, raw):
    @pl.when(leads())
    def _():
        wide = side_by_side(p_sum)
        for place, merged in enumerate((own, other)):
            raw[place] = jnp.dot(wide, merged[...], preferred_element_type=F32).astype(BF16)

    @pl.when(jnp.logical_not(leads()))
    def _():
        raw[...] = jnp.zeros_like(raw)


def raw_factors(p_sum, own, other):
    rows, columns = own.shape
    rank = p_sum.shape[1]
    return pl.pallas_call(
        raw_kernel,
        in_specs=[WHOLE] * 3,
        out_specs=WHOLE,
        out_shape=pltpu.VMEM((CORES, rank, columns), BF16),
        compiler_params=params(),
        cost_estimate=pl.CostEstimate(flops=4 * rank * rows * columns, bytes_accessed=4 * rows * columns, transcendentals=0),
        name="raw_factors",
    )(in_vmem(p_sum), in_vmem(own), in_vmem(other))


def turn_kernel(p_sum, gram, turned):
    blocks, rank, lanes = p_sum.shape
    wide = side_by_side(p_sum)
    gram[...] = lax.dot_general(wide, wide, (((1,), (1,)), ((), ())), preferred_element_type=F32)
    for block in range(blocks):
        tall = wide[:, block * lanes : (block + 1) * lanes].astype(F32).T.astype(BF16)
        turned[pl.ds(block * lanes, lanes), :] = jnp.concatenate([tall, tall], axis=1)


def turn(p_sum):
    blocks, rank, lanes = p_sum.shape
    return pl.pallas_call(
        turn_kernel,
        in_specs=[WHOLE],
        out_specs=[WHOLE, WHOLE],
        out_shape=[pltpu.VMEM((rank, rank), F32), pltpu.VMEM((blocks * lanes, 2 * rank), BF16)],
        compiler_params=params(),
        cost_estimate=pl.CostEstimate(flops=8 * rank * rank * blocks * lanes, bytes_accessed=2 << 20, transcendentals=0),
        name="turn",
    )(in_vmem(p_sum))


def solve_kernel(gram, inverse):
    rank = gram.shape[0]
    row = lax.broadcasted_iota(jnp.int32, (rank, rank), 0)
    col = lax.broadcasted_iota(jnp.int32, (rank, rank), 1)
    one = (row == col).astype(F32)
    table = jnp.concatenate([gram[...], one], axis=1)
    below = lax.broadcasted_iota(jnp.int32, (rank, 1), 0)
    for k in range(rank):
        pivot = table[k : k + 1, :]
        factor = jnp.where(below > k, table[:, k : k + 1] / pivot[:, k : k + 1], 0.0)
        table = table - factor * pivot
    diagonal = jnp.sum(table[:, :rank] * one, axis=1, keepdims=True)
    inverse[...] = table[:, rank:] * lax.rsqrt(diagonal)


def solve(gram):
    return pl.pallas_call(
        solve_kernel,
        in_specs=[WHOLE],
        out_specs=WHOLE,
        out_shape=pltpu.VMEM(gram.shape, F32),
        compiler_params=params(),
        cost_estimate=pl.CostEstimate(flops=8 << 20, bytes_accessed=4 << 20, transcendentals=0),
        name="solve",
    )(in_vmem(gram))


def finish_rows(replicas, raw, inverse, turned, merged, new_error, q_factor, halves, result, factor_out, done):
    factor = jnp.dot(inverse[...], raw[...], precision=HIGHEST, preferred_element_type=F32) * (1.0 / replicas)
    factor_out[...] = factor
    copies = [pltpu.make_async_copy(factor_out, q_factor, done.at[merged.shape[0] // STEP])]
    copies[0].start()
    rounded = factor.astype(BF16).astype(F32)
    solved = lax.dot_general(
        inverse[...], rounded, (((0,), (0,)), ((), ())), precision=HIGHEST, preferred_element_type=F32
    )
    high = solved.astype(BF16)
    halves[...] = jnp.concatenate([high, (solved - high.astype(F32)).astype(BF16)], axis=0)
    for chunk in range(merged.shape[0] // STEP):
        here = rows_of(chunk)
        rebuilt = jnp.dot(turned[here, :], halves[...], preferred_element_type=F32)
        result[here, :] = (merged[here, :].astype(F32) - rebuilt).astype(BF16)
        copies.append(pltpu.make_async_copy(result.at[here, :], new_error.at[0, here, :], done.at[chunk]))
        copies[-1].start()
    for copy in copies:
        copy.wait()


def first_kernel(replicas, *refs):
    @pl.when(leads())
    def _():
        finish_rows(replicas, *refs)


def second_kernel(replicas, raw, inverse, turned, merged, new_error_in, q_factor_in, *refs):
    @pl.when(jnp.logical_not(leads()))
    def _():
        finish_rows(replicas, raw, inverse, turned, merged, *refs)


def finish(raw, inverse, turned, merged, replicas, *begun):
    rows, columns = merged.shape
    rank = inverse.shape[0]
    kernel = second_kernel if begun else first_kernel
    return pl.pallas_call(
        lambda *refs: kernel(replicas, *refs),
        in_specs=[WHOLE] * 4 + [ANYWHERE] * len(begun),
        out_specs=[ANYWHERE] * 2,
        out_shape=[pltpu.HBM((1, rows, columns), BF16), pltpu.HBM((rank, columns), F32)],
        input_output_aliases={4 + i: i for i in range(len(begun))},
        scratch_shapes=[
            pltpu.VMEM((2 * rank, columns), BF16),
            pltpu.VMEM((rows, columns), BF16),
            pltpu.VMEM((rank, columns), F32),
            pltpu.SemaphoreType.DMA((rows // STEP + 1,)),
        ],
        compiler_params=params(),
        cost_estimate=pl.CostEstimate(flops=4 * rank * rows * columns, bytes_accessed=4 * rows * columns, transcendentals=0),
        name="finish_other" if begun else "finish_leading",
    )(*(in_vmem(x) for x in (raw, inverse, turned, merged)), *(in_hbm(x) for x in begun))


def exchange(blocks, axis, groups=None):
    return lax.all_to_all(blocks, axis, 0, 0, axis_index_groups=groups, tiled=True)


def share(block, axis, groups=None):
    count = len(groups[0]) if groups else lax.axis_size(axis)
    return exchange(jnp.broadcast_to(block[None], (count,) + block.shape), axis, groups)


def swap_cores(block):
    return lax.ppermute(block, "col", [(i, i ^ 1) for i in range(lax.axis_size("col"))])


def swap_chips(block, mask):
    columns, replicas = lax.axis_size("col"), lax.axis_size("rep")
    beside = columns // 4
    pairs = []
    for c in range(columns):
        for r in range(replicas):
            partner = (c, r ^ mask) if c % CORES else (c ^ beside, r)
            pairs.append((c * replicas + r, partner[0] * replicas + partner[1]))
    return lax.ppermute(block, ("col", "rep"), pairs)


def total(blocks):
    terms = [block.astype(F32) for block in blocks]
    while len(terms) > 1:
        terms = [a + b for a, b in zip(terms[::2], terms[1::2])]
    return terms[0]


def left_factor(part):
    chips = [list(range(c, lax.axis_size("col"), CORES)) for c in range(CORES)]
    count = len(chips[0])
    blocks = exchange(part, "col", chips)
    own = total(blocks.reshape((count, -1) + blocks.shape[1:])).astype(BF16)
    own = total(share(own, "rep")).astype(BF16)
    return share(own, "col", chips).reshape(part.shape)


def per_device(gradient, error, warm_start):
    replicas = lax.axis_size("rep")
    merged, part = merge(gradient, error, warm_start)
    handed, merged = lax.optimization_barrier((swap_cores(part), merged))
    part = total([part, handed]).astype(BF16)
    other = swap_cores(merged)
    p_sum = left_factor(part)
    raw = raw_factors(p_sum, merged, other)
    gram, turned = turn(p_sum)
    near = [swap_chips(raw, mask) for mask in (1, 2, 3)]
    raw, gram, *near = lax.optimization_barrier((raw, gram, *near))
    raw = total([raw, *near]).astype(BF16)
    far, inverse = lax.optimization_barrier((swap_chips(raw, 6), solve(gram)))
    raw = total([raw, far])
    begun = finish(raw[0], inverse, turned, merged, replicas)
    return tuple(finish(swap_cores(raw[1]), inverse, turned, merged, replicas, *begun))


def solution(mesh):
    in_specs = (P("rep", None, "col"), P("rep", None, "col"), P(None, "col"))
    out_specs = (P("rep", None, "col"), P(None, "col"))
    return jax.shard_map(
        per_device, mesh=mesh, in_specs=in_specs, out_specs=out_specs, check_vma=False
    )
```

```python
import jax
import jax.numpy as jnp
from jax import lax
from jax.experimental import pallas as pl
from jax.experimental.pallas import tpu as pltpu
from jax.sharding import PartitionSpec as P

BF16, F32 = jnp.bfloat16, jnp.float32
HIGHEST = lax.Precision.HIGHEST
LANES = 128
STEP = 512
WHOLE = pl.BlockSpec(memory_space=pltpu.VMEM)
ANYWHERE = pl.BlockSpec(memory_space=pl.ANY)


def params():
    return pltpu.CompilerParams(vmem_limit_bytes=40 << 20)


def in_vmem(array):
    return pltpu.with_memory_space_constraint(array, pltpu.VMEM)


def in_hbm(array):
    return pltpu.with_memory_space_constraint(array, pltpu.HBM)


def rows_of(chunk):
    return pl.ds(chunk * STEP, STEP)


def merge_kernel(gradient, error, warm, merged, part, gradient_in, error_in, warm_in, done):
    chunks = merged.shape[0] // STEP
    copies = [pltpu.make_async_copy(warm, warm_in, done.at[2 * chunks])]
    for chunk in range(chunks):
        here = rows_of(chunk)
        copies.append(pltpu.make_async_copy(gradient.at[0, here, :], gradient_in.at[here, :], done.at[2 * chunk]))
        copies.append(pltpu.make_async_copy(error.at[0, here, :], error_in.at[here, :], done.at[2 * chunk + 1]))
    for copy in copies:
        copy.start()
    copies[0].wait()
    for chunk in range(chunks):
        here = rows_of(chunk)
        copies[2 * chunk + 1].wait()
        copies[2 * chunk + 2].wait()
        value = (gradient_in[here, :].astype(F32) + error_in[here, :].astype(F32)).astype(BF16)
        merged[here, :] = value
        product = lax.dot_general(warm_in[...], value, (((1,), (1,)), ((), ())), preferred_element_type=F32)
        for block in range(STEP // LANES):
            part[chunk * (STEP // LANES) + block] = product[:, block * LANES : (block + 1) * LANES].astype(BF16)


def merge(gradient, error, warm):
    _, rows, columns = gradient.shape
    rank = warm.shape[0]
    return pl.pallas_call(
        merge_kernel,
        in_specs=[ANYWHERE] * 3,
        out_specs=[WHOLE, WHOLE],
        out_shape=[
            pltpu.VMEM((rows, columns), BF16),
            pltpu.VMEM((rows // LANES, rank, LANES), BF16),
        ],
        scratch_shapes=[
            pltpu.VMEM((rows, columns), BF16),
            pltpu.VMEM((rows, columns), BF16),
            pltpu.VMEM((rank, columns), BF16),
            pltpu.SemaphoreType.DMA((2 * (rows // STEP) + 1,)),
        ],
        compiler_params=params(),
        cost_estimate=pl.CostEstimate(flops=2 * rank * rows * columns, bytes_accessed=4 * rows * columns, transcendentals=0),
        name="merge",
    )(in_hbm(gradient), in_hbm(error), in_hbm(warm))


def side_by_side(blocks):
    return jnp.concatenate([blocks[i] for i in range(blocks.shape[0])], axis=1)


def raw_kernel(p_sum, merged, raw):
    raw[...] = jnp.dot(side_by_side(p_sum), merged[...], preferred_element_type=F32).astype(BF16)


def raw_factor(p_sum, merged):
    rows, columns = merged.shape
    rank = p_sum.shape[1]
    return pl.pallas_call(
        raw_kernel,
        in_specs=[WHOLE, WHOLE],
        out_specs=WHOLE,
        out_shape=pltpu.VMEM((rank, columns), BF16),
        compiler_params=params(),
        cost_estimate=pl.CostEstimate(flops=2 * rank * rows * columns, bytes_accessed=2 * rows * columns, transcendentals=0),
        name="raw_factor",
    )(in_vmem(p_sum), in_vmem(merged))


def turn_kernel(p_sum, gram, turned):
    blocks, rank, lanes = p_sum.shape
    wide = side_by_side(p_sum)
    gram[...] = lax.dot_general(wide, wide, (((1,), (1,)), ((), ())), preferred_element_type=F32)
    for block in range(blocks):
        tall = wide[:, block * lanes : (block + 1) * lanes].astype(F32).T.astype(BF16)
        turned[pl.ds(block * lanes, lanes), :] = jnp.concatenate([tall, tall], axis=1)


def turn(p_sum):
    blocks, rank, lanes = p_sum.shape
    return pl.pallas_call(
        turn_kernel,
        in_specs=[WHOLE],
        out_specs=[WHOLE, WHOLE],
        out_shape=[pltpu.VMEM((rank, rank), F32), pltpu.VMEM((blocks * lanes, 2 * rank), BF16)],
        compiler_params=params(),
        cost_estimate=pl.CostEstimate(flops=8 * rank * rank * blocks * lanes, bytes_accessed=2 << 20, transcendentals=0),
        name="turn",
    )(in_vmem(p_sum))


def solve_kernel(gram, inverse):
    rank = gram.shape[0]
    row = lax.broadcasted_iota(jnp.int32, (rank, rank), 0)
    col = lax.broadcasted_iota(jnp.int32, (rank, rank), 1)
    one = (row == col).astype(F32)
    table = jnp.concatenate([gram[...], one], axis=1)
    below = lax.broadcasted_iota(jnp.int32, (rank, 1), 0)
    for k in range(rank):
        pivot = table[k : k + 1, :]
        factor = jnp.where(below > k, table[:, k : k + 1] / pivot[:, k : k + 1], 0.0)
        table = table - factor * pivot
    diagonal = jnp.sum(table[:, :rank] * one, axis=1, keepdims=True)
    inverse[...] = table[:, rank:] * lax.rsqrt(diagonal)


def solve(gram):
    return pl.pallas_call(
        solve_kernel,
        in_specs=[WHOLE],
        out_specs=WHOLE,
        out_shape=pltpu.VMEM(gram.shape, F32),
        compiler_params=params(),
        cost_estimate=pl.CostEstimate(flops=8 << 20, bytes_accessed=4 << 20, transcendentals=0),
        name="solve",
    )(in_vmem(gram))


def finish_kernel(replicas, mine, theirs, inverse, turned, merged, new_error, q_factor, halves, result, factor_out, done):
    raw = mine[...].astype(F32) + theirs[...].astype(F32)
    factor = jnp.dot(inverse[...], raw, precision=HIGHEST, preferred_element_type=F32) * (1.0 / replicas)
    factor_out[...] = factor
    copies = [pltpu.make_async_copy(factor_out, q_factor, done.at[merged.shape[0] // STEP])]
    copies[0].start()
    rounded = factor.astype(BF16).astype(F32)
    solved = lax.dot_general(
        inverse[...], rounded, (((0,), (0,)), ((), ())), precision=HIGHEST, preferred_element_type=F32
    )
    high = solved.astype(BF16)
    halves[...] = jnp.concatenate([high, (solved - high.astype(F32)).astype(BF16)], axis=0)
    for chunk in range(merged.shape[0] // STEP):
        here = rows_of(chunk)
        rebuilt = jnp.dot(turned[here, :], halves[...], preferred_element_type=F32)
        result[here, :] = (merged[here, :].astype(F32) - rebuilt).astype(BF16)
        copies.append(pltpu.make_async_copy(result.at[here, :], new_error.at[0, here, :], done.at[chunk]))
        copies[-1].start()
    for copy in copies:
        copy.wait()


def finish(mine, theirs, inverse, turned, merged, replicas):
    rows, columns = merged.shape
    rank = inverse.shape[0]
    return pl.pallas_call(
        lambda *refs: finish_kernel(replicas, *refs),
        in_specs=[WHOLE] * 5,
        out_specs=[ANYWHERE] * 2,
        out_shape=[pltpu.HBM((1, rows, columns), BF16), pltpu.HBM((rank, columns), F32)],
        scratch_shapes=[
            pltpu.VMEM((2 * rank, columns), BF16),
            pltpu.VMEM((rows, columns), BF16),
            pltpu.VMEM((rank, columns), F32),
            pltpu.SemaphoreType.DMA((rows // STEP + 1,)),
        ],
        compiler_params=params(),
        cost_estimate=pl.CostEstimate(flops=4 * rank * rows * columns, bytes_accessed=4 * rows * columns, transcendentals=0),
        name="finish",
    )(*(in_vmem(x) for x in (mine, theirs, inverse, turned, merged)))


def exchange(blocks, axis):
    return lax.all_to_all(blocks, axis, 0, 0, tiled=True)


def share(block, axis):
    return exchange(jnp.broadcast_to(block[None], (lax.axis_size(axis),) + block.shape), axis)


def total(blocks):
    terms = [block.astype(F32) for block in blocks]
    while len(terms) > 1:
        terms = [a + b for a, b in zip(terms[::2], terms[1::2])]
    return terms[0]


def swap(block, axis, mask):
    return lax.ppermute(block, axis, [(i, i ^ mask) for i in range(lax.axis_size(axis))])


def per_device(gradient, error, warm_start):
    replicas = lax.axis_size("rep")
    merged, part = merge(gradient, error, warm_start)
    own = total(exchange(part, "col"))
    own = total(share(own.astype(BF16), "rep"))
    p_sum = share(own.astype(BF16), "col")
    raw = raw_factor(p_sum, merged)
    gram, turned = turn(p_sum)
    near = [swap(raw, "rep", mask) for mask in (1, 2, 3)]
    raw, gram, *near = lax.optimization_barrier((raw, gram, *near))
    raw = total([raw, *near]).astype(BF16)
    far, inverse = lax.optimization_barrier((swap(raw, "rep", 6), solve(gram)))
    return tuple(finish(raw, far, inverse, turned, merged, replicas))


def solution(mesh):
    in_specs = (P("rep", None, "col"), P("rep", None, "col"), P(None, "col"))
    out_specs = (P("rep", None, "col"), P(None, "col"))
    return jax.shard_map(
        per_device, mesh=mesh, in_specs=in_specs, out_specs=out_specs, check_vma=False
    )
```

```python
import jax
import jax.numpy as jnp
from jax import lax
from jax.experimental import pallas as pl
from jax.experimental.pallas import tpu as pltpu
from jax.sharding import PartitionSpec as P

BF16, F32 = jnp.bfloat16, jnp.float32
HIGHEST = lax.Precision.HIGHEST
LATE = {"col": 21, "rep": 5}
LANES = 128
STEP = 512
WHOLE = pl.BlockSpec(memory_space=pltpu.VMEM)
ANYWHERE = pl.BlockSpec(memory_space=pl.ANY)


def params():
    return pltpu.CompilerParams(vmem_limit_bytes=40 << 20)


def in_vmem(array):
    return pltpu.with_memory_space_constraint(array, pltpu.VMEM)


def in_hbm(array):
    return pltpu.with_memory_space_constraint(array, pltpu.HBM)


def rows_of(chunk):
    return pl.ds(chunk * STEP, STEP)


def merge_kernel(gradient, error, warm, merged, part, gradient_in, error_in, warm_in, done):
    chunks = merged.shape[0] // STEP
    copies = [pltpu.make_async_copy(warm, warm_in, done.at[2 * chunks])]
    for chunk in range(chunks):
        here = rows_of(chunk)
        copies.append(pltpu.make_async_copy(gradient.at[0, here, :], gradient_in.at[here, :], done.at[2 * chunk]))
        copies.append(pltpu.make_async_copy(error.at[0, here, :], error_in.at[here, :], done.at[2 * chunk + 1]))
    for copy in copies:
        copy.start()
    copies[0].wait()
    for chunk in range(chunks):
        here = rows_of(chunk)
        copies[2 * chunk + 1].wait()
        copies[2 * chunk + 2].wait()
        value = (gradient_in[here, :].astype(F32) + error_in[here, :].astype(F32)).astype(BF16)
        merged[here, :] = value
        product = lax.dot_general(warm_in[...], value, (((1,), (1,)), ((), ())), preferred_element_type=F32)
        for block in range(STEP // LANES):
            part[chunk * (STEP // LANES) + block] = product[:, block * LANES : (block + 1) * LANES].astype(BF16)


def merge(gradient, error, warm):
    _, rows, columns = gradient.shape
    rank = warm.shape[0]
    return pl.pallas_call(
        merge_kernel,
        in_specs=[ANYWHERE] * 3,
        out_specs=[WHOLE, WHOLE],
        out_shape=[
            pltpu.VMEM((rows, columns), BF16),
            pltpu.VMEM((rows // LANES, rank, LANES), BF16),
        ],
        scratch_shapes=[
            pltpu.VMEM((rows, columns), BF16),
            pltpu.VMEM((rows, columns), BF16),
            pltpu.VMEM((rank, columns), BF16),
            pltpu.SemaphoreType.DMA((2 * (rows // STEP) + 1,)),
        ],
        compiler_params=params(),
        cost_estimate=pl.CostEstimate(flops=2 * rank * rows * columns, bytes_accessed=4 * rows * columns, transcendentals=0),
        name="merge",
    )(in_hbm(gradient), in_hbm(error), in_hbm(warm))


def side_by_side(blocks):
    return jnp.concatenate([blocks[i] for i in range(blocks.shape[0])], axis=1)


def raw_kernel(p_sum, merged, raw):
    raw[...] = jnp.dot(side_by_side(p_sum), merged[...], preferred_element_type=F32).astype(BF16)


def raw_factor(p_sum, merged):
    rows, columns = merged.shape
    rank = p_sum.shape[1]
    return pl.pallas_call(
        raw_kernel,
        in_specs=[WHOLE, WHOLE],
        out_specs=WHOLE,
        out_shape=pltpu.VMEM((rank, columns), BF16),
        compiler_params=params(),
        cost_estimate=pl.CostEstimate(flops=2 * rank * rows * columns, bytes_accessed=2 * rows * columns, transcendentals=0),
        name="raw_factor",
    )(in_vmem(p_sum), in_vmem(merged))


def turn_kernel(p_sum, gram, turned):
    blocks, rank, lanes = p_sum.shape
    wide = side_by_side(p_sum)
    gram[...] = lax.dot_general(wide, wide, (((1,), (1,)), ((), ())), preferred_element_type=F32)
    for block in range(blocks):
        tall = wide[:, block * lanes : (block + 1) * lanes].astype(F32).T.astype(BF16)
        turned[pl.ds(block * lanes, lanes), :] = jnp.concatenate([tall, tall], axis=1)


def turn(p_sum):
    blocks, rank, lanes = p_sum.shape
    return pl.pallas_call(
        turn_kernel,
        in_specs=[WHOLE],
        out_specs=[WHOLE, WHOLE],
        out_shape=[pltpu.VMEM((rank, rank), F32), pltpu.VMEM((blocks * lanes, 2 * rank), BF16)],
        compiler_params=params(),
        cost_estimate=pl.CostEstimate(flops=8 * rank * rank * blocks * lanes, bytes_accessed=2 << 20, transcendentals=0),
        name="turn",
    )(in_vmem(p_sum))


def solve_kernel(gram, inverse):
    rank = gram.shape[0]
    row = lax.broadcasted_iota(jnp.int32, (rank, rank), 0)
    col = lax.broadcasted_iota(jnp.int32, (rank, rank), 1)
    one = (row == col).astype(F32)
    table = jnp.concatenate([gram[...], one], axis=1)
    below = lax.broadcasted_iota(jnp.int32, (rank, 1), 0)
    for k in range(rank):
        pivot = table[k : k + 1, :]
        factor = jnp.where(below > k, table[:, k : k + 1] / pivot[:, k : k + 1], 0.0)
        table = table - factor * pivot
    diagonal = jnp.sum(table[:, :rank] * one, axis=1, keepdims=True)
    inverse[...] = table[:, rank:] * lax.rsqrt(diagonal)


def solve(gram):
    return pl.pallas_call(
        solve_kernel,
        in_specs=[WHOLE],
        out_specs=WHOLE,
        out_shape=pltpu.VMEM(gram.shape, F32),
        compiler_params=params(),
        cost_estimate=pl.CostEstimate(flops=8 << 20, bytes_accessed=4 << 20, transcendentals=0),
        name="solve",
    )(in_vmem(gram))


def finish_kernel(replicas, mine, theirs, inverse, turned, merged, new_error, q_factor, halves, result, factor_out, done):
    raw = mine[...].astype(F32) + theirs[...].astype(F32)
    factor = jnp.dot(inverse[...], raw, precision=HIGHEST, preferred_element_type=F32) * (1.0 / replicas)
    factor_out[...] = factor
    copies = [pltpu.make_async_copy(factor_out, q_factor, done.at[merged.shape[0] // STEP])]
    copies[0].start()
    rounded = factor.astype(BF16).astype(F32)
    solved = lax.dot_general(
        inverse[...], rounded, (((0,), (0,)), ((), ())), precision=HIGHEST, preferred_element_type=F32
    )
    high = solved.astype(BF16)
    halves[...] = jnp.concatenate([high, (solved - high.astype(F32)).astype(BF16)], axis=0)
    for chunk in range(merged.shape[0] // STEP):
        here = rows_of(chunk)
        rebuilt = jnp.dot(turned[here, :], halves[...], preferred_element_type=F32)
        result[here, :] = (merged[here, :].astype(F32) - rebuilt).astype(BF16)
        copies.append(pltpu.make_async_copy(result.at[here, :], new_error.at[0, here, :], done.at[chunk]))
        copies[-1].start()
    for copy in copies:
        copy.wait()


def finish(mine, theirs, inverse, turned, merged, replicas):
    rows, columns = merged.shape
    rank = inverse.shape[0]
    return pl.pallas_call(
        lambda *refs: finish_kernel(replicas, *refs),
        in_specs=[WHOLE] * 5,
        out_specs=[ANYWHERE] * 2,
        out_shape=[pltpu.HBM((1, rows, columns), BF16), pltpu.HBM((rank, columns), F32)],
        scratch_shapes=[
            pltpu.VMEM((2 * rank, columns), BF16),
            pltpu.VMEM((rows, columns), BF16),
            pltpu.VMEM((rank, columns), F32),
            pltpu.SemaphoreType.DMA((rows // STEP + 1,)),
        ],
        compiler_params=params(),
        cost_estimate=pl.CostEstimate(flops=4 * rank * rows * columns, bytes_accessed=4 * rows * columns, transcendentals=0),
        name="finish",
    )(*(in_vmem(x) for x in (mine, theirs, inverse, turned, merged)))


def exchange(blocks, axis):
    places = list(range(lax.axis_size(axis)))
    first = LATE[axis]
    return lax.all_to_all(blocks, axis, 0, 0, axis_index_groups=[places[first:] + places[:first]], tiled=True)


def share(block, axis):
    return exchange(jnp.broadcast_to(block[None], (lax.axis_size(axis),) + block.shape), axis)


def total(blocks):
    terms = [block.astype(F32) for block in blocks]
    while len(terms) > 1:
        terms = [a + b for a, b in zip(terms[::2], terms[1::2])]
    return terms[0]


def swap(block, axis, mask):
    return lax.ppermute(block, axis, [(i, i ^ mask) for i in range(lax.axis_size(axis))])


def per_device(gradient, error, warm_start):
    replicas = lax.axis_size("rep")
    merged, part = merge(gradient, error, warm_start)
    own = total(exchange(part, "col"))
    own = total(share(own.astype(BF16), "rep"))
    p_sum = share(own.astype(BF16), "col")
    raw = raw_factor(p_sum, merged)
    gram, turned = turn(p_sum)
    near = [swap(raw, "rep", mask) for mask in (1, 2, 3)]
    raw, gram, *near = lax.optimization_barrier((raw, gram, *near))
    raw = total([raw, *near]).astype(BF16)
    far, inverse = lax.optimization_barrier((swap(raw, "rep", 6), solve(gram)))
    return tuple(finish(raw, far, inverse, turned, merged, replicas))


def solution(mesh):
    in_specs = (P("rep", None, "col"), P("rep", None, "col"), P(None, "col"))
    out_specs = (P("rep", None, "col"), P(None, "col"))
    return jax.shard_map(
        per_device, mesh=mesh, in_specs=in_specs, out_specs=out_specs, check_vma=False
    )
```

```python
import math

import jax
import jax.numpy as jnp
from jax import lax
from jax.experimental import pallas as pl
from jax.experimental.pallas import tpu as pltpu
from jax.sharding import PartitionSpec as P

BF16, F32 = jnp.bfloat16, jnp.float32
HIGHEST = lax.Precision.HIGHEST
CORES = 2
LATE = {"col": 21, "rep": 5}
LANES = 128
STEP = 512
WHOLE = pl.BlockSpec(memory_space=pltpu.VMEM)
ANYWHERE = pl.BlockSpec(memory_space=pl.ANY)


def params():
    return pltpu.CompilerParams(vmem_limit_bytes=40 << 20)


def in_vmem(array):
    return pltpu.with_memory_space_constraint(array, pltpu.VMEM)


def in_hbm(array):
    return pltpu.with_memory_space_constraint(array, pltpu.HBM)


def rows_of(chunk):
    return pl.ds(chunk * STEP, STEP)


def merge_kernel(gradient, error, warm, merged, part, gradient_in, error_in, warm_in, done):
    chunks = merged.shape[0] // STEP
    copies = [pltpu.make_async_copy(warm, warm_in, done.at[2 * chunks])]
    for chunk in range(chunks):
        here = rows_of(chunk)
        copies.append(pltpu.make_async_copy(gradient.at[0, here, :], gradient_in.at[here, :], done.at[2 * chunk]))
        copies.append(pltpu.make_async_copy(error.at[0, here, :], error_in.at[here, :], done.at[2 * chunk + 1]))
    for copy in copies:
        copy.start()
    copies[0].wait()
    for chunk in range(chunks):
        here = rows_of(chunk)
        copies[2 * chunk + 1].wait()
        copies[2 * chunk + 2].wait()
        value = (gradient_in[here, :].astype(F32) + error_in[here, :].astype(F32)).astype(BF16)
        merged[here, :] = value
        product = lax.dot_general(warm_in[...], value, (((1,), (1,)), ((), ())), preferred_element_type=F32)
        for block in range(STEP // LANES):
            part[chunk * (STEP // LANES) + block] = product[:, block * LANES : (block + 1) * LANES].astype(BF16)


def merge(gradient, error, warm):
    _, rows, columns = gradient.shape
    rank = warm.shape[0]
    return pl.pallas_call(
        merge_kernel,
        in_specs=[ANYWHERE] * 3,
        out_specs=[WHOLE, WHOLE],
        out_shape=[
            pltpu.VMEM((rows, columns), BF16),
            pltpu.VMEM((rows // LANES, rank, LANES), BF16),
        ],
        scratch_shapes=[
            pltpu.VMEM((rows, columns), BF16),
            pltpu.VMEM((rows, columns), BF16),
            pltpu.VMEM((rank, columns), BF16),
            pltpu.SemaphoreType.DMA((2 * (rows // STEP) + 1,)),
        ],
        compiler_params=params(),
        cost_estimate=pl.CostEstimate(flops=2 * rank * rows * columns, bytes_accessed=4 * rows * columns, transcendentals=0),
        name="merge",
    )(in_hbm(gradient), in_hbm(error), in_hbm(warm))


def side_by_side(blocks):
    return jnp.concatenate([blocks[i] for i in range(blocks.shape[0])], axis=1)


def raw_kernel(p_sum, merged, raw):
    raw[...] = jnp.dot(side_by_side(p_sum), merged[...], preferred_element_type=F32).astype(BF16)


def raw_factor(p_sum, merged):
    rows, columns = merged.shape
    rank = p_sum.shape[1]
    return pl.pallas_call(
        raw_kernel,
        in_specs=[WHOLE, WHOLE],
        out_specs=WHOLE,
        out_shape=pltpu.VMEM((rank, columns), BF16),
        compiler_params=params(),
        cost_estimate=pl.CostEstimate(flops=2 * rank * rows * columns, bytes_accessed=2 * rows * columns, transcendentals=0),
        name="raw_factor",
    )(in_vmem(p_sum), in_vmem(merged))


def turn_kernel(p_sum, gram, turned):
    blocks, rank, lanes = p_sum.shape
    wide = side_by_side(p_sum)
    gram[...] = lax.dot_general(wide, wide, (((1,), (1,)), ((), ())), preferred_element_type=F32)
    for block in range(blocks):
        tall = wide[:, block * lanes : (block + 1) * lanes].astype(F32).T.astype(BF16)
        turned[pl.ds(block * lanes, lanes), :] = jnp.concatenate([tall, tall], axis=1)


def turn(p_sum):
    blocks, rank, lanes = p_sum.shape
    return pl.pallas_call(
        turn_kernel,
        in_specs=[WHOLE],
        out_specs=[WHOLE, WHOLE],
        out_shape=[pltpu.VMEM((rank, rank), F32), pltpu.VMEM((blocks * lanes, 2 * rank), BF16)],
        compiler_params=params(),
        cost_estimate=pl.CostEstimate(flops=8 * rank * rank * blocks * lanes, bytes_accessed=2 << 20, transcendentals=0),
        name="turn",
    )(in_vmem(p_sum))


def solve_kernel(gram, inverse):
    rank = gram.shape[0]
    row = lax.broadcasted_iota(jnp.int32, (rank, rank), 0)
    col = lax.broadcasted_iota(jnp.int32, (rank, rank), 1)
    one = (row == col).astype(F32)
    table = jnp.concatenate([gram[...], one], axis=1)
    below = lax.broadcasted_iota(jnp.int32, (rank, 1), 0)
    for k in range(rank):
        pivot = table[k : k + 1, :]
        factor = jnp.where(below > k, table[:, k : k + 1] / pivot[:, k : k + 1], 0.0)
        table = table - factor * pivot
    diagonal = jnp.sum(table[:, :rank] * one, axis=1, keepdims=True)
    inverse[...] = table[:, rank:] * lax.rsqrt(diagonal)


def solve(gram):
    return pl.pallas_call(
        solve_kernel,
        in_specs=[WHOLE],
        out_specs=WHOLE,
        out_shape=pltpu.VMEM(gram.shape, F32),
        compiler_params=params(),
        cost_estimate=pl.CostEstimate(flops=8 << 20, bytes_accessed=4 << 20, transcendentals=0),
        name="solve",
    )(in_vmem(gram))


def finish_kernel(replicas, mine, theirs, inverse, turned, merged, new_error, q_factor, halves, result, factor_out, done):
    raw = mine[...].astype(F32) + theirs[...].astype(F32)
    factor = jnp.dot(inverse[...], raw, precision=HIGHEST, preferred_element_type=F32) * (1.0 / replicas)
    factor_out[...] = factor
    copies = [pltpu.make_async_copy(factor_out, q_factor, done.at[merged.shape[0] // STEP])]
    copies[0].start()
    rounded = factor.astype(BF16).astype(F32)
    solved = lax.dot_general(
        inverse[...], rounded, (((0,), (0,)), ((), ())), precision=HIGHEST, preferred_element_type=F32
    )
    high = solved.astype(BF16)
    halves[...] = jnp.concatenate([high, (solved - high.astype(F32)).astype(BF16)], axis=0)
    for chunk in range(merged.shape[0] // STEP):
        here = rows_of(chunk)
        rebuilt = jnp.dot(turned[here, :], halves[...], preferred_element_type=F32)
        result[here, :] = (merged[here, :].astype(F32) - rebuilt).astype(BF16)
        copies.append(pltpu.make_async_copy(result.at[here, :], new_error.at[0, here, :], done.at[chunk]))
        copies[-1].start()
    for copy in copies:
        copy.wait()


def finish(mine, theirs, inverse, turned, merged, replicas):
    rows, columns = merged.shape
    rank = inverse.shape[0]
    return pl.pallas_call(
        lambda *refs: finish_kernel(replicas, *refs),
        in_specs=[WHOLE] * 5,
        out_specs=[ANYWHERE] * 2,
        out_shape=[pltpu.HBM((1, rows, columns), BF16), pltpu.HBM((rank, columns), F32)],
        scratch_shapes=[
            pltpu.VMEM((2 * rank, columns), BF16),
            pltpu.VMEM((rows, columns), BF16),
            pltpu.VMEM((rank, columns), F32),
            pltpu.SemaphoreType.DMA((rows // STEP + 1,)),
        ],
        compiler_params=params(),
        cost_estimate=pl.CostEstimate(flops=4 * rank * rows * columns, bytes_accessed=4 * rows * columns, transcendentals=0),
        name="finish",
    )(*(in_vmem(x) for x in (mine, theirs, inverse, turned, merged)))


def hops(axis, place):
    first, size = LATE[axis], lax.axis_size(axis)
    rings = [(place, first, size)]
    if axis == "col":
        along = math.isqrt(size // CORES)
        rings = [(p // CORES // along, f // CORES // along, along) for p, f, _ in rings]
        rings.append((place // CORES % along, first // CORES % along, along))
    return sum(min((p - f) % n, (f - p) % n) for p, f, n in rings)


def exchange(blocks, axis):
    places = sorted(range(lax.axis_size(axis)), key=lambda p: (p != LATE[axis], hops(axis, p), -(p % CORES), p))
    return lax.all_to_all(blocks, axis, 0, 0, axis_index_groups=[places], tiled=True)


def share(block, axis):
    return exchange(jnp.broadcast_to(block[None], (lax.axis_size(axis),) + block.shape), axis)


def total(blocks):
    terms = [block.astype(F32) for block in blocks]
    while len(terms) > 1:
        terms = [a + b for a, b in zip(terms[::2], terms[1::2])]
    return terms[0]


def swap(block, axis, mask):
    return lax.ppermute(block, axis, [(i, i ^ mask) for i in range(lax.axis_size(axis))])


def per_device(gradient, error, warm_start):
    replicas = lax.axis_size("rep")
    merged, part = merge(gradient, error, warm_start)
    own = total(exchange(part, "col"))
    own = total(share(own.astype(BF16), "rep"))
    p_sum = share(own.astype(BF16), "col")
    raw = raw_factor(p_sum, merged)
    gram, turned = turn(p_sum)
    near = [swap(raw, "rep", mask) for mask in (1, 2, 3)]
    raw, gram, *near = lax.optimization_barrier((raw, gram, *near))
    raw = total([raw, *near]).astype(BF16)
    far, inverse = lax.optimization_barrier((swap(raw, "rep", 6), solve(gram)))
    return tuple(finish(raw, far, inverse, turned, merged, replicas))


def solution(mesh):
    in_specs = (P("rep", None, "col"), P("rep", None, "col"), P(None, "col"))
    out_specs = (P("rep", None, "col"), P(None, "col"))
    return jax.shard_map(
        per_device, mesh=mesh, in_specs=in_specs, out_specs=out_specs, check_vma=False
    )
```

```python
import math

import jax
import jax.numpy as jnp
from jax import lax
from jax.experimental import pallas as pl
from jax.experimental.pallas import tpu as pltpu
from jax.sharding import PartitionSpec as P

BF16, F32 = jnp.bfloat16, jnp.float32
HIGHEST = lax.Precision.HIGHEST
CORES = 2
LATE = {"col": 21, "rep": 5}
LANES = 128
STEP = 512
WHOLE = pl.BlockSpec(memory_space=pltpu.VMEM)
ANYWHERE = pl.BlockSpec(memory_space=pl.ANY)


def params():
    return pltpu.CompilerParams(vmem_limit_bytes=40 << 20)


def in_vmem(array):
    return pltpu.with_memory_space_constraint(array, pltpu.VMEM)


def in_hbm(array):
    return pltpu.with_memory_space_constraint(array, pltpu.HBM)


def rows_of(chunk):
    return pl.ds(chunk * STEP, STEP)


def merge_kernel(gradient, error, warm, merged, part, gradient_in, error_in, warm_in, done):
    chunks = merged.shape[0] // STEP
    copies = [pltpu.make_async_copy(warm, warm_in, done.at[2 * chunks])]
    for chunk in range(chunks):
        here = rows_of(chunk)
        copies.append(pltpu.make_async_copy(gradient.at[0, here, :], gradient_in.at[here, :], done.at[2 * chunk]))
        copies.append(pltpu.make_async_copy(error.at[0, here, :], error_in.at[here, :], done.at[2 * chunk + 1]))
    for copy in copies:
        copy.start()
    copies[0].wait()
    for chunk in range(chunks):
        here = rows_of(chunk)
        copies[2 * chunk + 1].wait()
        copies[2 * chunk + 2].wait()
        value = (gradient_in[here, :].astype(F32) + error_in[here, :].astype(F32)).astype(BF16)
        merged[here, :] = value
        product = lax.dot_general(warm_in[...], value, (((1,), (1,)), ((), ())), preferred_element_type=F32)
        for block in range(STEP // LANES):
            part[chunk * (STEP // LANES) + block] = product[:, block * LANES : (block + 1) * LANES].astype(BF16)


def merge(gradient, error, warm):
    _, rows, columns = gradient.shape
    rank = warm.shape[0]
    return pl.pallas_call(
        merge_kernel,
        in_specs=[ANYWHERE] * 3,
        out_specs=[WHOLE, WHOLE],
        out_shape=[
            pltpu.VMEM((rows, columns), BF16),
            pltpu.VMEM((rows // LANES, rank, LANES), BF16),
        ],
        scratch_shapes=[
            pltpu.VMEM((rows, columns), BF16),
            pltpu.VMEM((rows, columns), BF16),
            pltpu.VMEM((rank, columns), BF16),
            pltpu.SemaphoreType.DMA((2 * (rows // STEP) + 1,)),
        ],
        compiler_params=params(),
        cost_estimate=pl.CostEstimate(flops=2 * rank * rows * columns, bytes_accessed=4 * rows * columns, transcendentals=0),
        name="merge",
    )(in_hbm(gradient), in_hbm(error), in_hbm(warm))


def side_by_side(blocks):
    return jnp.concatenate([blocks[i] for i in range(blocks.shape[0])], axis=1)


def raw_kernel(p_sum, merged, raw):
    raw[...] = jnp.dot(side_by_side(p_sum), merged[...], preferred_element_type=F32).astype(BF16)


def raw_factor(p_sum, merged):
    rows, columns = merged.shape
    rank = p_sum.shape[1]
    return pl.pallas_call(
        raw_kernel,
        in_specs=[WHOLE, WHOLE],
        out_specs=WHOLE,
        out_shape=pltpu.VMEM((rank, columns), BF16),
        compiler_params=params(),
        cost_estimate=pl.CostEstimate(flops=2 * rank * rows * columns, bytes_accessed=2 * rows * columns, transcendentals=0),
        name="raw_factor",
    )(in_vmem(p_sum), in_vmem(merged))


def turn_kernel(p_sum, gram, turned):
    blocks, rank, lanes = p_sum.shape
    wide = side_by_side(p_sum)
    gram[...] = lax.dot_general(wide, wide, (((1,), (1,)), ((), ())), preferred_element_type=F32)
    for block in range(blocks):
        tall = wide[:, block * lanes : (block + 1) * lanes].astype(F32).T.astype(BF16)
        turned[pl.ds(block * lanes, lanes), :] = jnp.concatenate([tall, tall], axis=1)


def turn(p_sum):
    blocks, rank, lanes = p_sum.shape
    return pl.pallas_call(
        turn_kernel,
        in_specs=[WHOLE],
        out_specs=[WHOLE, WHOLE],
        out_shape=[pltpu.VMEM((rank, rank), F32), pltpu.VMEM((blocks * lanes, 2 * rank), BF16)],
        compiler_params=params(),
        cost_estimate=pl.CostEstimate(flops=8 * rank * rank * blocks * lanes, bytes_accessed=2 << 20, transcendentals=0),
        name="turn",
    )(in_vmem(p_sum))


def solve_kernel(gram, inverse):
    rank = gram.shape[0]
    row = lax.broadcasted_iota(jnp.int32, (rank, rank), 0)
    col = lax.broadcasted_iota(jnp.int32, (rank, rank), 1)
    one = (row == col).astype(F32)
    table = jnp.concatenate([gram[...], one], axis=1)
    below = lax.broadcasted_iota(jnp.int32, (rank, 1), 0)
    for k in range(rank):
        pivot = table[k : k + 1, :]
        factor = jnp.where(below > k, table[:, k : k + 1] / pivot[:, k : k + 1], 0.0)
        table = table - factor * pivot
    diagonal = jnp.sum(table[:, :rank] * one, axis=1, keepdims=True)
    inverse[...] = table[:, rank:] * lax.rsqrt(diagonal)


def solve(gram):
    return pl.pallas_call(
        solve_kernel,
        in_specs=[WHOLE],
        out_specs=WHOLE,
        out_shape=pltpu.VMEM(gram.shape, F32),
        compiler_params=params(),
        cost_estimate=pl.CostEstimate(flops=8 << 20, bytes_accessed=4 << 20, transcendentals=0),
        name="solve",
    )(in_vmem(gram))


def terms_of(value, count):
    terms = []
    for _ in range(count):
        terms.append(value.astype(BF16))
        value = value - terms[-1].astype(F32)
    return terms


def finish_kernel(replicas, mine, theirs, inverse, turned, merged, new_error, q_factor, halves, result, factor_out, done):
    raw = terms_of(mine[...].astype(F32) + theirs[...].astype(F32), 2)
    lower = terms_of(inverse[...], 3)
    factor = jnp.dot(jnp.concatenate(lower, axis=1), jnp.concatenate([raw[0]] * 3), preferred_element_type=F32)
    factor += jnp.dot(jnp.concatenate(lower[:2], axis=1), jnp.concatenate([raw[1]] * 2), preferred_element_type=F32)
    factor *= 1.0 / replicas
    factor_out[...] = factor
    copies = [pltpu.make_async_copy(factor_out, q_factor, done.at[merged.shape[0] // STEP])]
    copies[0].start()
    rounded = factor.astype(BF16)
    solved = lax.dot_general(
        jnp.concatenate(lower), jnp.concatenate([rounded] * 3), (((0,), (0,)), ((), ())), preferred_element_type=F32
    )
    high = solved.astype(BF16)
    halves[...] = jnp.concatenate([high, (solved - high.astype(F32)).astype(BF16)], axis=0)
    for chunk in range(merged.shape[0] // STEP):
        here = rows_of(chunk)
        rebuilt = jnp.dot(turned[here, :], halves[...], preferred_element_type=F32)
        result[here, :] = (merged[here, :].astype(F32) - rebuilt).astype(BF16)
        copies.append(pltpu.make_async_copy(result.at[here, :], new_error.at[0, here, :], done.at[chunk]))
        copies[-1].start()
    for copy in copies:
        copy.wait()


def finish(mine, theirs, inverse, turned, merged, replicas):
    rows, columns = merged.shape
    rank = inverse.shape[0]
    return pl.pallas_call(
        lambda *refs: finish_kernel(replicas, *refs),
        in_specs=[WHOLE] * 5,
        out_specs=[ANYWHERE] * 2,
        out_shape=[pltpu.HBM((1, rows, columns), BF16), pltpu.HBM((rank, columns), F32)],
        scratch_shapes=[
            pltpu.VMEM((2 * rank, columns), BF16),
            pltpu.VMEM((rows, columns), BF16),
            pltpu.VMEM((rank, columns), F32),
            pltpu.SemaphoreType.DMA((rows // STEP + 1,)),
        ],
        compiler_params=params(),
        cost_estimate=pl.CostEstimate(flops=4 * rank * rows * columns, bytes_accessed=4 * rows * columns, transcendentals=0),
        name="finish",
    )(*(in_vmem(x) for x in (mine, theirs, inverse, turned, merged)))


def hops(axis, place):
    first, size = LATE[axis], lax.axis_size(axis)
    rings = [(place, first, size)]
    if axis == "col":
        along = math.isqrt(size // CORES)
        rings = [(p // CORES // along, f // CORES // along, along) for p, f, _ in rings]
        rings.append((place // CORES % along, first // CORES % along, along))
    return sum(min((p - f) % n, (f - p) % n) for p, f, n in rings)


def exchange(blocks, axis):
    places = sorted(range(lax.axis_size(axis)), key=lambda p: (p != LATE[axis], hops(axis, p), -(p % CORES), p))
    return lax.all_to_all(blocks, axis, 0, 0, axis_index_groups=[places], tiled=True)


def share(block, axis):
    return exchange(jnp.broadcast_to(block[None], (lax.axis_size(axis),) + block.shape), axis)


def total(blocks):
    terms = [block.astype(F32) for block in blocks]
    while len(terms) > 1:
        terms = [a + b for a, b in zip(terms[::2], terms[1::2])]
    return terms[0]


def swap(block, axis, mask):
    return lax.ppermute(block, axis, [(i, i ^ mask) for i in range(lax.axis_size(axis))])


def per_device(gradient, error, warm_start):
    replicas = lax.axis_size("rep")
    merged, part = merge(gradient, error, warm_start)
    own = total(exchange(part, "col"))
    own = total(share(own.astype(BF16), "rep"))
    p_sum = share(own.astype(BF16), "col")
    raw = raw_factor(p_sum, merged)
    gram, turned = turn(p_sum)
    near = [swap(raw, "rep", mask) for mask in (1, 2, 3)]
    raw, gram, *near = lax.optimization_barrier((raw, gram, *near))
    raw = total([raw, *near]).astype(BF16)
    far, inverse = lax.optimization_barrier((swap(raw, "rep", 6), solve(gram)))
    return tuple(finish(raw, far, inverse, turned, merged, replicas))


def solution(mesh):
    in_specs = (P("rep", None, "col"), P("rep", None, "col"), P(None, "col"))
    out_specs = (P("rep", None, "col"), P(None, "col"))
    return jax.shard_map(
        per_device, mesh=mesh, in_specs=in_specs, out_specs=out_specs, check_vma=False
    )
```
